256 devices in a mesh: ctx: 32 (over z, y_lo, core), head: 8 (over y_hi, x).
Axes of the slice: x: 4, y: 4 (y_hi: 2, y_lo: 2; y = y_hi * 2 + y_lo), z: 8, core: 2. Of those that a mesh axis runs over, the one named last changes fastest.
Arguments:
- q_nope: bfloat16 [4096, 8192], P('ctx', 'head'), may hold values from -6 to 6
- q_rope: bfloat16 [4096, 4096], P('ctx', 'head'), may hold values from -6 to 6
- latent_keys: bfloat16 [4096, 576], P('ctx'), may hold values from -128 to 128
- kv_gain: float32 [512], replicated, may hold values from 0.5 to 2
- up_key: bfloat16 [512, 8192], P(None, 'head'), may hold values from -0.25 to 0.25
- up_value: bfloat16 [512, 8192], P(None, 'head'), may hold values from -0.25 to 0.25
- out_proj: bfloat16 [8192, 7168], P('head', 'ctx'), may hold values from -0.5 to 0.5
- block_order: int32 [64], replicated, may hold values from 0 to 63, each once
Outputs:
- mixed: bfloat16 [4096, 7168], P('ctx', 'head')
The draws below stay inside these ranges and needn't reach their ends.
Inputs may be any that keep to these rules, and one draw needn't show every extreme that they name: `block_order`: each stored block gets a different sequence block.
All inputs are finite; a program needn't handle non-finite values.
Results may differ from the reference program's by a relative error of at most 0.017.
Values may be sent and summed in bfloat16 or wider, within the bound.
A program may use at most 128 MiB of HBM per device.

```python
import math
import jax
import jax.numpy as jnp
from jax import lax

D = 7168
HEADS = 64
NOPE = 128
ROPE = 64
VDIM = 128
LATENT = 512
HALF = 64
SEQ = 4096
BLOCKS = 64


def draw_q_rope(key, part):
    key = jax.random.fold_in(key, 1)
    values = jnp.clip(1.5 * jax.random.normal(key, (SEQ, HEADS * ROPE), jnp.float32), -6.0, 6.0)
    return values.astype(jnp.bfloat16)


def draw_latent_keys(key, part):
    key = jax.random.fold_in(key, 2)
    values = jnp.clip(jax.random.normal(key, (SEQ, LATENT + ROPE), jnp.float32), -6.0, 6.0)
    return values.astype(jnp.bfloat16)


def block_scale(stream_key, dims, shards, least, high):
    level, own = 1.0, jax.random.fold_in(stream_key, 6)
    for dim, parts in shards:
        heights = jnp.exp(jax.random.uniform(jax.random.fold_in(own, dim), (parts,), jnp.float32, least / len(shards), high / len(shards)))
        level = level * jnp.repeat(heights, dims[dim] // parts).reshape([-1 if axis == dim else 1 for axis in range(len(dims))])
    return level


def noise(key, shape, spread, bound, cuts=(), kind=jnp.bfloat16):
    result = jax.random.normal(key, shape, jnp.float32) * spread
    if len(cuts) > 0:
        result = block_scale(key, shape, cuts, -0.22, 0.18) * result
    return jnp.clip(result, min=-bound, max=bound).astype(kind)


def setup_inputs(seed: int = 0) -> dict:
    seeds = jax.random.split(jax.random.key(seed), 9)
    return {
        "q_nope": noise(seeds[0], (SEQ, HEADS * NOPE), 1.5, 6.0, ((0, 32), (1, 8))),
        "q_rope": draw_q_rope(jax.random.fold_in(seeds[8], 71), 0),
        "latent_keys": draw_latent_keys(jax.random.fold_in(seeds[8], 71), 0),
        "kv_gain": jnp.clip(jnp.exp(jax.random.uniform(seeds[3], (LATENT,), jnp.float32, math.log(0.5), math.log(2.0))), 0.5, 2.0),
        "up_key": noise(seeds[4], (LATENT, HEADS * NOPE), LATENT ** -0.5, 0.25, ((1, 8),)),
        "up_value": noise(seeds[5], (LATENT, HEADS * VDIM), LATENT ** -0.5, 0.25, ((1, 8),)),
        "out_proj": noise(seeds[6], (HEADS * VDIM, D), (HEADS * VDIM // 64) ** -0.5, 0.5, ((0, 8), (1, 32))),
        "block_order": jax.random.permutation(seeds[7], BLOCKS).astype(jnp.int32),
    }


def normalize_latent(latent_keys, kv_gain):
    latent = latent_keys[:, :LATENT].astype(jnp.float32)
    inverse = lax.rsqrt(lax.optimization_barrier(jnp.mean(latent * latent, axis=1, keepdims=True)) + 1e-06)
    return (latent * inverse * kv_gain.astype(jnp.float32)[None, :]).astype(jnp.bfloat16)

def reference(q_nope, q_rope, latent_keys, kv_gain, up_key, up_value, out_proj, block_order):
    highest = lax.Precision.HIGHEST
    normed = normalize_latent(latent_keys, kv_gain)
    rope_key = latent_keys[:, LATENT:]
    keys = jnp.dot(normed, up_key, preferred_element_type=jnp.float32).reshape(SEQ, HEADS, NOPE)
    values = jnp.dot(normed, up_value, preferred_element_type=jnp.float32).reshape(SEQ, HEADS, VDIM)
    row_index = jnp.arange(SEQ, dtype=jnp.int32)
    position = block_order[row_index // HALF] * HALF + row_index % HALF
    visible = position[None, :] <= position[:, None]
    query_nope = q_nope.astype(jnp.float32).reshape(SEQ, HEADS, NOPE)
    query_rope = q_rope.reshape(SEQ, HEADS, ROPE)
    factor = 1.0 / (NOPE + ROPE) ** 0.5

    def one_head(head_id):
        score = jnp.dot(query_nope[:, head_id, :], keys[:, head_id, :].T, precision=highest, preferred_element_type=jnp.float32)
        score = score + jnp.dot(query_rope[:, head_id, :], rope_key.T, preferred_element_type=jnp.float32)
        score = jnp.where(visible, score * factor, -jnp.inf)
        peak = lax.optimization_barrier(jnp.max(score, axis=1, keepdims=True))
        expo = jnp.exp(score - peak)
        total = lax.optimization_barrier(jnp.sum(expo, axis=1, keepdims=True))
        weight = lax.optimization_barrier(expo.astype(jnp.bfloat16)).astype(jnp.float32)
        summed = jnp.dot(weight, values[:, head_id, :], precision=highest, preferred_element_type=jnp.float32)
        return (summed / total).astype(jnp.bfloat16)
    heads_out = lax.map(one_head, jnp.arange(HEADS, dtype=jnp.int32))
    attended = jnp.transpose(heads_out, (1, 0, 2)).reshape(SEQ, HEADS * VDIM)
    return jnp.dot(attended, out_proj, preferred_element_type=jnp.float32).astype(jnp.bfloat16)
```

```python
import functools
import math

import jax
import jax.numpy as jnp
from jax import lax
from jax.experimental import pallas as pl
from jax.experimental.pallas import tpu as pltpu
from jax.sharding import PartitionSpec as P

NOPE = 128
ROPE = 64
VDIM = 128
LATENT = 512
WIDTH = 640
NZ = 8
NQ = 4
NX = 4
NH = 8
HIDDEN = -1e30
SCALE = math.log2(math.e) / (NOPE + ROPE) ** 0.5
MESH = pl.DeviceIdType.MESH
F32 = jnp.float32
BF16 = jnp.bfloat16


def dot(a, b, dims=((1,), (0,))):
    return lax.dot_general(a, b, (dims, ((), ())), preferred_element_type=F32)


def slots_of(step):
    if step == 0:
        return (0,)
    if step == NZ // 2:
        return (step,)
    return (step, NZ - step)


def kernel(
    order, gain, latent, qn_hbm, qr_hbm, upk_hbm, upv_hbm, w_hbm, out,
    qn, qr, upk, upv, wbuf, kbuf, qbuf, acc, top, total, abuf, pbuf, rsbuf, red, tbuf, obuf,
    load_sem, kz_send, kz_recv, kc_send, kc_recv, ky_send, ky_recv, kd_send, kd_recv,
    w_send, w_recv, az_send, az_recv, rs_send, rs_recv, t_send, t_recv, o_send, o_recv,
):
    rows = latent.shape[0]
    half = rows // 2
    heads = upk.shape[1] // NOPE
    cols = wbuf.shape[2]
    part = rows // NH
    ctx = lax.axis_index("ctx")
    head = lax.axis_index("head")
    z, q = lax.div(ctx, NQ), lax.rem(ctx, NQ)
    y_lo, core = lax.div(q, 2), lax.rem(q, 2)
    y_hi, x = lax.div(head, NX), lax.rem(head, NX)
    q_core = q + 1 - 2 * core
    q_y = lax.rem(q + 2, NQ)
    q_diag = q_y + 1 - 2 * core
    quads = (q, q_core, q_y, q_diag)

    def along_z(step):
        return lax.rem(z + step + NZ, NZ) * NQ + q, head

    def in_plane(step):
        return ctx, lax.rem(head + step, NH)

    to_core = (z * NQ + q_core, head)
    to_y = (z * NQ + q_y, head)
    to_up = (z * NQ + q_y, lax.rem(y_hi + y_lo, 2) * NX + x)
    to_down = (z * NQ + q_y, lax.rem(y_hi + 1 - y_lo, 2) * NX + x)

    def send(src, dst, send_sem, recv_sem, device):
        return pltpu.make_async_remote_copy(
            src_ref=src, dst_ref=dst, send_sem=send_sem, recv_sem=recv_sem,
            device_id=device, device_id_type=MESH,
        )

    loads = [
        pltpu.make_async_copy(src, dst, load_sem.at[n])
        for n, (src, dst) in enumerate(
            ((qn_hbm, qn), (upk_hbm, upk), (qr_hbm, qr), (upv_hbm, upv), (w_hbm, wbuf.at[q]))
        )
    ]
    for load in loads:
        load.start()

    partners = [along_z(n) for n in range(1, NZ)] + [in_plane(n) for n in range(1, NH)]
    partners += [to_core, to_up, to_down]
    barrier = pltpu.get_barrier_semaphore()
    for device in partners:
        pl.semaphore_signal(barrier, inc=1, device_id=device, device_id_type=MESH)

    plain = latent[:, :LATENT].astype(F32)
    inverse = lax.rsqrt(jnp.mean(plain * plain, axis=1, keepdims=True) + 1e-06)
    kbuf[0, 0, :, :LATENT] = (plain * inverse * gain[...]).astype(BF16)
    kbuf[0, 0, :, LATENT:] = jnp.concatenate(
        [latent[:, LATENT:], jnp.zeros((rows, WIDTH - LATENT - ROPE), BF16)], axis=1
    )
    pl.semaphore_wait(barrier, len(partners))

    def ring(view, send_sem, recv_sem, way, step):
        source = (NZ - step) % NZ if way == 0 else step
        target = (NZ - step - 1) % NZ if way == 0 else step + 1
        src, dst = view(source), view(target)
        if step == NZ // 2 - 1:
            piece = pl.ds(way * half, half)
            src, dst = src.at[piece], dst.at[piece]
        return send(src, dst, send_sem.at[way, step], recv_sem.at[way, step], along_z(1 - 2 * way))

    k_ring = functools.partial(ring, lambda slot: kbuf.at[slot, 0], kz_send, kz_recv)
    a_ring = functools.partial(ring, lambda slot: abuf.at[slot], az_send, az_recv)

    def k_core(slot):
        return send(kbuf.at[slot, 0], kbuf.at[slot, 1], kc_send.at[slot], kc_recv.at[slot], to_core)

    def k_y(slot, way):
        piece = pl.ds(way * half, half)
        return send(
            kbuf.at[slot, 0, piece], kbuf.at[slot, 2, piece],
            ky_send.at[way, slot], ky_recv.at[way, slot], (to_down, to_up)[way],
        )

    def k_diag(slot):
        return send(kbuf.at[slot, 2], kbuf.at[slot, 3], kd_send.at[slot], kd_recv.at[slot], to_core)

    w_core = send(w_hbm, wbuf.at[q], w_send.at[0], w_recv.at[0], to_core)
    w_y = send(w_hbm, wbuf.at[q], w_send.at[1], w_recv.at[1], to_y)
    w_diag = send(wbuf.at[q_y], wbuf.at[q_y], w_send.at[2], w_recv.at[2], to_core)

    last = NZ // 2

    def comm(t):
        if t <= last:
            if t > 0:
                for way in range(2):
                    k_ring(way, t - 1).wait_recv()
            if t < last:
                for way in range(2):
                    k_ring(way, t).start()
            for slot in slots_of(t):
                k_y(slot, 0).start()
                k_y(slot, 1).start()
                k_core(slot).start()
        if 1 <= t <= last + 1:
            for slot in slots_of(t - 1):
                k_y(slot, 0).wait_recv()
                k_y(slot, 1).wait_recv()
                k_diag(slot).start()
        if t >= 2:
            for slot in slots_of(t - 2):
                k_core(slot).wait_recv()
                k_diag(slot).wait_recv()

    comm(0)

    loads[0].wait()
    loads[1].wait()
    loads[2].wait()
    for n in range(heads):
        span = slice(n * rows, (n + 1) * rows)
        own = slice(n * NOPE, (n + 1) * NOPE)
        qbuf[span, :LATENT] = dot(qn[:, own], upk[:, own], ((1,), (1,))).astype(BF16)
        qbuf[span, LATENT:] = jnp.concatenate(
            [qr[:, n * ROPE : (n + 1) * ROPE], jnp.zeros((rows, WIDTH - LATENT - ROPE), BF16)],
            axis=1,
        )
    acc[...] = jnp.zeros_like(acc)
    total[...] = jnp.zeros_like(total)
    top[...] = jnp.full_like(top, HIDDEN)

    comm(1)
    w_y.start()
    w_core.start()

    def places(block, axis):
        shape = (rows, 1) if axis == 0 else (1, rows)
        index = lax.broadcasted_iota(jnp.int32, shape, axis)
        first, second = order[2 * block], order[2 * block + 1]
        return jnp.where(index < half, first * half + index, (second - 1) * half + index)

    query_place = places(ctx, 0)
    chunk = 2 * rows
    keys = NQ * rows

    def attend(i, carry):
        for t, when in ((2, 0), (3, 1), (4, 3), (5, 5), (6, 7)):
            pl.when(i == when)(functools.partial(comm, t))
        slot = jnp.where(lax.rem(i, 2) == 1, lax.div(i + 1, 2), lax.rem(NZ - lax.div(i, 2), NZ))
        from_z = lax.rem(z + slot, NZ) * NQ
        key_place = jnp.concatenate([places(from_z + quad, 1) for quad in quads], axis=1)
        visible = key_place <= query_place
        visible = jnp.concatenate([visible] * (chunk // rows), axis=0)
        for r in range(heads * rows // chunk):
            span = slice(r * chunk, (r + 1) * chunk)
            block = kbuf[slot].reshape(keys, WIDTH)
            score = jnp.where(visible, dot(qbuf[span], block, ((1,), (1,))), HIDDEN)
            before = top[span]
            peak = jnp.maximum(before, jnp.max(score, axis=1, keepdims=True))
            fade = jnp.exp2((before - peak) * SCALE)
            expo = jnp.exp2((score - jnp.concatenate([peak] * (keys // 128), axis=1)) * SCALE)
            part_sum = expo[:, :128]
            for n in range(1, keys // 128):
                part_sum = part_sum + expo[:, n * 128 : (n + 1) * 128]
            total[span] = total[span] * fade + part_sum
            top[span] = peak
            faded = acc[span] * jnp.concatenate([fade] * (LATENT // 128), axis=1)
            acc[span] = faded + dot(expo.astype(BF16), block[:, :LATENT])
        return carry

    lax.fori_loop(0, NZ, attend, 0)

    loads[3].wait()
    for n in range(heads):
        span = slice(n * rows, (n + 1) * rows)
        own = slice(n * VDIM, (n + 1) * VDIM)
        wide = acc[span]
        high = wide.astype(BF16)
        low = (wide - high.astype(F32)).astype(BF16)
        summed = dot(high, upv[:, own]) + dot(low, upv[:, own])
        abuf[0, :, own] = (summed / jnp.sum(total[span], axis=1, keepdims=True)).astype(BF16)

    for way in range(2):
        a_ring(way, 0).start()
    w_y.wait_recv()
    w_diag.start()
    loads[4].wait()
    w_core.wait_recv()
    w_diag.wait_recv()

    def scatter(slot, step):
        first = pl.multiple_of(lax.rem(head + step, NH) * part, part)
        return send(
            pbuf.at[slot, pl.ds(first, part)], rsbuf.at[slot, step - 1],
            rs_send.at[slot, step - 1], rs_recv.at[slot, step - 1], in_plane(step),
        )

    def home(slot):
        return send(
            red.at[slot], tbuf.at[(NZ - slot) % NZ],
            t_send.at[slot], t_recv.at[(NZ - slot) % NZ], along_z(slot),
        )

    mine = pl.ds(pl.multiple_of(head * part, part), part)

    def place(slot):
        target = lax.rem(z + slot, NZ)
        n = lax.rem(target - head + NH, NH)
        return target, send(tbuf.at[slot], obuf.at[mine], o_send.at[n], o_recv.at[n], (ctx, target))

    def project(t):
        if t <= last:
            if t > 0:
                for way in range(2):
                    a_ring(way, t - 1).wait_recv()
            if 0 < t < last:
                for way in range(2):
                    a_ring(way, t).start()
            lanes = slots_of(t)
            rows_in = abuf[lanes[0]]
            if len(lanes) > 1:
                rows_in = jnp.concatenate([abuf[slot] for slot in lanes], axis=0)
            for n in range(NQ):
                made = dot(rows_in, wbuf[n]).astype(BF16)
                for m, slot in enumerate(lanes):
                    pbuf[slot, :, n * cols : (n + 1) * cols] = made[m * rows : (m + 1) * rows]
            for slot in lanes:
                for step in range(1, NH):
                    scatter(slot, step).start()
        if 1 <= t <= last + 1:
            for slot in slots_of(t - 1):
                value = pbuf[slot, mine].astype(F32)
                for step in range(1, NH):
                    scatter(slot, step).wait_recv()
                    value = value + rsbuf[slot, step - 1].astype(F32)
                if slot == 0:
                    tbuf[0] = value.astype(BF16)
                else:
                    red[slot] = value.astype(BF16)
                    home(slot).start()
        if t >= 2:
            for slot in slots_of(t - 2):
                if slot > 0:
                    home((NZ - slot) % NZ).wait_recv()
                target, copy = place(slot)
                pl.when(target != head)(copy.start)

                @pl.when(target == head)
                def _():
                    obuf[mine] = tbuf[slot]

    for t in range(last + 3):
        project(t)

    for n in range(1, NH):
        there = pl.ds(pl.multiple_of(lax.rem(head - n + NH, NH) * part, part), part)
        send(tbuf.at[0], obuf.at[there], o_send.at[n], o_recv.at[n], in_plane(n)).wait_recv()
    out[...] = obuf[...]

    for step in range(last):
        for way in range(2):
            k_ring(way, step).wait_send()
            a_ring(way, step).wait_send()
    for slot in range(NZ):
        k_core(slot).wait_send()
        k_diag(slot).wait_send()
        k_y(slot, 0).wait_send()
        k_y(slot, 1).wait_send()
        for step in range(1, NH):
            scatter(slot, step).wait_send()
        if slot > 0:
            home(slot).wait_send()
    for n in range(1, NH):
        send(tbuf.at[0], obuf.at[mine], o_send.at[n], o_recv.at[n], in_plane(n)).wait_send()
    w_core.wait_send()
    w_y.wait_send()
    w_diag.wait_send()


def per_device(q_nope, q_rope, latent_keys, kv_gain, up_key, up_value, out_proj, block_order):
    rows = q_nope.shape[0]
    heads = up_key.shape[1] // NOPE
    depth, cols = out_proj.shape
    wide = NQ * cols
    dma = pltpu.SemaphoreType.DMA
    vmem = pl.BlockSpec(memory_space=pltpu.VMEM)
    hbm = pl.BlockSpec(memory_space=pl.ANY)
    return pl.pallas_call(
        kernel,
        out_shape=jax.ShapeDtypeStruct((rows, wide), BF16),
        in_specs=[pl.BlockSpec(memory_space=pltpu.SMEM), vmem, vmem] + [hbm] * 5,
        out_specs=vmem,
        scratch_shapes=[
            pltpu.VMEM(q_nope.shape, BF16),
            pltpu.VMEM(q_rope.shape, BF16),
            pltpu.VMEM(up_key.shape, BF16),
            pltpu.VMEM(up_value.shape, BF16),
            pltpu.VMEM((NQ, depth, cols), BF16),
            pltpu.VMEM((NZ, NQ, rows, WIDTH), BF16),
            pltpu.VMEM((heads * rows, WIDTH), BF16),
            pltpu.VMEM((heads * rows, LATENT), F32),
            pltpu.VMEM((heads * rows, 128), F32),
            pltpu.VMEM((heads * rows, 128), F32),
            pltpu.VMEM((NZ, rows, heads * VDIM), BF16),
            pltpu.VMEM((NZ, rows, wide), BF16),
            pltpu.VMEM((NZ, NH - 1, rows // NH, wide), BF16),
            pltpu.VMEM((NZ, rows // NH, wide), BF16),
            pltpu.VMEM((NZ, rows // NH, wide), BF16),
            pltpu.VMEM((rows, wide), BF16),
            dma((5,)),
            dma((2, NZ // 2)), dma((2, NZ // 2)),
            dma((NZ,)), dma((NZ,)),
            dma((2, NZ)), dma((2, NZ)),
            dma((NZ,)), dma((NZ,)),
            dma((3,)), dma((3,)),
            dma((2, NZ // 2)), dma((2, NZ // 2)),
            dma((NZ, NH - 1)), dma((NZ, NH - 1)),
            dma((NZ,)), dma((NZ,)),
            dma((NH,)), dma((NH,)),
        ],
        compiler_params=pltpu.CompilerParams(
            collective_id=0, has_side_effects=True, vmem_limit_bytes=56 * 1024 * 1024
        ),
    )(
        block_order, kv_gain.reshape(1, LATENT), latent_keys,
        q_nope, q_rope, up_key, up_value, out_proj,
    )


def solution(mesh):
    return jax.shard_map(
        per_device,
        mesh=mesh,
        in_specs=(
            P("ctx", "head"),
            P("ctx", "head"),
            P("ctx", None),
            P(),
            P(None, "head"),
            P(None, "head"),
            P("head", "ctx"),
            P(),
        ),
        out_specs=P("ctx", "head"),
        check_vma=False,
    )
```

```python
import math

import jax
import jax.numpy as jnp
from jax import lax
from jax.experimental import pallas as pl
from jax.experimental.pallas import tpu as pltpu
from jax.sharding import PartitionSpec as P

NOPE = 128
ROPE = 64
VDIM = 128
LATENT = 512
CARRIED = LATENT + ROPE
BLOCKS = 64
WIDTH = CARRIED + BLOCKS
NZ = 8
NQ = 4
NX = 4
NH = 8
HIDDEN = -1e30
SCALE = math.log2(math.e) / (NOPE + ROPE) ** 0.5
MESH = pl.DeviceIdType.MESH
F32 = jnp.float32
BF16 = jnp.bfloat16

Z_PIECES = ((0, 192), (192, 192), (384, 192))
Z_LAST = (((0, 192), (192, 96), None), (None, (288, 96), (384, 192)))
HALF_WIDTH = CARRIED // 2
Y_PIECES = ((0, 192), (192, 96))
X_PIECES = ((0, 144), (144, 144))
UNITS = ((0, 1, 0), (7, 2, 0), (6, 3, 0), (0, 1, 1), (5, 4, 0), (7, 2, 1), (6, 3, 1), (5, 4, 1))


def dot(a, b, dims=((1,), (0,))):
    return lax.dot_general(a, b, (dims, ((), ())), preferred_element_type=F32)


def slots_of(step):
    if step == 0:
        return (0,)
    if step == NZ // 2:
        return (step,)
    return (step, NZ - step)


def pick(table, i):
    value = jnp.int32(table[0])
    for n in range(1, len(table)):
        value = jnp.where(i == n, table[n], value)
    return value


def kernel(
    order, gain, latent, qn_hbm, qr_hbm, upk_hbm, upv_hbm, w_hbm, out,
    qn, qr, upk, upv, wbuf, kbuf, qbuf, acc, top, total, tri, abuf, pbuf, rsbuf, red, obuf,
    load_sem, kz_send, kz_recv, kc_send, kc_recv, ky_send, ky_recv, kx_send, kx_recv,
    kd_send, kd_recv, w_send, w_recv, az_send, az_recv, rs_send, rs_recv, t_send, t_recv,
):
    rows = latent.shape[1]
    half = rows // 2
    heads = upk.shape[1] // NOPE
    cols, depth = w_hbm.shape
    part = rows // NH
    last = NZ // 2
    ctx = lax.axis_index("ctx")
    head = lax.axis_index("head")
    z, q = lax.div(ctx, NQ), lax.rem(ctx, NQ)
    y_lo, core = lax.div(q, 2), lax.rem(q, 2)
    y_hi, x = lax.div(head, NX), lax.rem(head, NX)
    x_odd = lax.rem(x, 2)
    q_core = q + 1 - 2 * core
    q_y = lax.rem(q + 2, NQ)
    q_diag = q_y + 1 - 2 * core
    quads = (q, q_core, q_y, q_diag)

    def along_z(step):
        return lax.rem(z + step + NZ, NZ) * NQ + q, head

    def along_x(step):
        return ctx, y_hi * NX + lax.rem(x + step + NX, NX)

    to_core = (z * NQ + q_core, head)
    to_near = (z * NQ + q_y, head)
    to_far = (z * NQ + q_y, lax.rem(y_hi + 1, 2) * NX + x)

    def send(src, dst, send_sem, recv_sem, device):
        return pltpu.make_async_remote_copy(
            src_ref=src, dst_ref=dst, send_sem=send_sem, recv_sem=recv_sem,
            device_id=device, device_id_type=MESH,
        )

    loads = [
        pltpu.make_async_copy(src, dst, load_sem.at[n])
        for n, (src, dst) in enumerate(
            ((qn_hbm, qn), (upk_hbm, upk), (qr_hbm, qr), (upv_hbm, upv), (w_hbm, wbuf.at[q]))
        )
    ]
    for load in loads:
        load.start()

    sources = [along_z(1), along_z(-1), to_core, to_near, to_far]
    sources += [(ctx, lax.rem(head + n, NH)) for n in range(1, NH)]
    barrier = pltpu.get_barrier_semaphore()
    for device in sources:
        pl.semaphore_signal(barrier, inc=1, device_id=device, device_id_type=MESH)
    for n in range(NH):
        device = (head * NQ + q, n)

        @pl.when(jnp.logical_or(z != head, head != n))
        def _():
            pl.semaphore_signal(barrier, inc=1, device_id=device, device_id_type=MESH)

    plain = latent[:LATENT].astype(F32)
    inverse = lax.rsqrt(jnp.mean(plain * plain, axis=0, keepdims=True) + 1e-06)
    for n in range(LATENT // 128):
        span = slice(n * 128, (n + 1) * 128)
        column = jnp.broadcast_to(gain[n : n + 1], (128, 128)).T
        kbuf[0, 0, span] = (plain[span] * inverse * column).astype(BF16)
    kbuf[0, 0, LATENT:CARRIED] = latent[LATENT:]

    which = lax.broadcasted_iota(jnp.int32, (BLOCKS, rows), 0)
    first_half = lax.broadcasted_iota(jnp.int32, (BLOCKS, rows), 1) < half

    def mark(slot, carry):
        from_z = lax.rem(z + slot, NZ) * NQ
        for n, quad in enumerate(quads):
            there = 2 * (from_z + quad)
            owner = jnp.where(first_half, order[there], order[there + 1])
            kbuf[slot, n, CARRIED:] = jnp.where(which == owner, 1.0, 0.0).astype(BF16)
        return carry

    lax.fori_loop(0, NZ, mark, 0)
    lane = lax.broadcasted_iota(jnp.int32, (half, BLOCKS), 1)
    for r in range(2):
        row = lax.broadcasted_iota(jnp.int32, (half, rows), 0)
        key = lax.broadcasted_iota(jnp.int32, (half, rows), 1) - r * half
        tri[r] = jnp.where(jnp.logical_and(key > row, key < half), HIDDEN, 0.0)
    acc[...] = jnp.zeros_like(acc)
    total[...] = jnp.zeros_like(total)
    top[...] = jnp.full_like(top, HIDDEN)

    def kz(way, step, k):
        source = (NZ - step) % NZ if way == 0 else step
        target = (NZ - step - 1) % NZ if way == 0 else step + 1
        piece = (Z_PIECES if step < last - 1 else Z_LAST[way])[k]
        span = pl.ds(*piece)
        return send(
            kbuf.at[source, 0, span], kbuf.at[target, 0, span],
            kz_send.at[way, step, k], kz_recv.at[way, step, k], along_z(1 - 2 * way),
        )

    def kc(slot):
        span = pl.ds(0, CARRIED)
        return send(
            kbuf.at[slot, 0, span], kbuf.at[slot, 1, span],
            kc_send.at[slot], kc_recv.at[slot], to_core,
        )

    def kept(odd, first, size):
        return pl.ds(pl.multiple_of(odd * HALF_WIDTH + first, 16), size)

    def ky(slot, n):
        span = kept(x_odd, *Y_PIECES[n])
        return send(
            kbuf.at[slot, 0, span], kbuf.at[slot, 2, span],
            ky_send.at[n, slot], ky_recv.at[n, slot], (to_far, to_near)[n],
        )

    def kx(slot, n, coming=False):
        span = kept(1 - x_odd if coming else x_odd, *X_PIECES[n])
        return send(
            kbuf.at[slot, 2, span], kbuf.at[slot, 2, span],
            kx_send.at[n, slot], kx_recv.at[n, slot], along_x(1 - 2 * n),
        )

    def kd(slot, n):
        span = kept(x_odd if n == 0 else 1 - x_odd, 0, HALF_WIDTH)
        return send(
            kbuf.at[slot, 2, span], kbuf.at[slot, 3, span],
            kd_send.at[n, slot], kd_recv.at[n, slot], to_core,
        )

    w_core = send(w_hbm, wbuf.at[q], w_send.at[0], w_recv.at[0], to_core)
    w_near = send(w_hbm, wbuf.at[q], w_send.at[1], w_recv.at[1], to_near)
    w_diag = send(wbuf.at[q_y], wbuf.at[q_y], w_send.at[2], w_recv.at[2], to_core)

    def z_pieces(step):
        return [
            (way, k)
            for n in range(3)
            for way, k in ((0, n), (1, 2 - n))
            if step < last - 1 or Z_LAST[way][k] is not None
        ]

    def share(step):
        for slot in slots_of(step):
            ky(slot, 0).start()
            ky(slot, 1).start()
        for slot in slots_of(step):
            kc(slot).start()

    def from_z(step, n):
        for way, k in ((0, n), (1, 2 - n)):
            if (way, k) in z_pieces(step - 1):
                kz(way, step - 1, k).wait_recv()
                if step < last and (way, k) in z_pieces(step):
                    kz(way, step, k).start()
        if n == (2 if step < last else 1):
            share(step)

    def from_y(step):
        for slot in slots_of(step):
            ky(slot, 0).wait_recv()
            ky(slot, 1).wait_recv()
            kx(slot, 0).start()
            kx(slot, 1).start()
            kd(slot, 0).start()

    def from_x(step):
        for slot in slots_of(step):
            kx(slot, 0, True).wait_recv()
            kx(slot, 1, True).wait_recv()
            kd(slot, 1).start()

    def near_core(*slots):
        for slot in slots:
            kc(slot).wait_recv()

    def far_core(*slots):
        for slot in slots:
            kd(slot, 0).wait_recv()
            kd(slot, 1).wait_recv()

    loads[0].wait()
    loads[1].wait()
    loads[2].wait()
    for n in range(heads):
        own = slice(n * NOPE, (n + 1) * NOPE)
        turned = dot(qn[:, own], upk[:, own], ((1,), (1,))).astype(BF16)
        rope = qr[:, n * ROPE : (n + 1) * ROPE]
        for r in range(2):
            span = slice((r * heads + n) * half, (r * heads + n + 1) * half)
            mine = slice(r * half, (r + 1) * half)
            later = jnp.where(lane > order[2 * ctx + r], HIDDEN, 0.0).astype(BF16)
            qbuf[span, :LATENT] = turned[mine]
            qbuf[span, LATENT:] = jnp.concatenate([rope[mine], later], axis=1)

    pl.semaphore_wait(barrier, len(sources) + NH - jnp.where(z == head, 1, 0))

    for way, k in z_pieces(0):
        kz(way, 0, k).start()
    share(0)
    w_core.start()
    from_z(1, 0)
    from_z(1, 1)
    from_z(1, 2)
    from_y(0)
    w_near.start()
    from_z(2, 0)

    def before_1():
        from_z(2, 1)
        from_z(2, 2)
        from_x(0)
        from_y(1)
        from_z(3, 0)
        near_core(7, 2)

    def before_2():
        from_z(3, 1)
        from_z(3, 2)
        from_x(1)
        from_y(2)
        from_z(4, 0)
        near_core(6, 3)

    def before_3():
        from_z(4, 1)
        far_core(0, 1)

    def before_4():
        from_x(2)
        from_y(3)
        near_core(5, 4)

    def before_5():
        from_y(4)
        from_x(3)
        far_core(7, 2)

    befores = (lambda: near_core(0, 1), before_1, before_2, before_3, before_4, before_5)
    chunk = heads * half

    def soft(span, score, block):
        keys = score.shape[1]
        before = top[span]
        peak = jnp.maximum(before, jnp.max(score, axis=1, keepdims=True))
        fade = jnp.exp2((before - peak) * SCALE)
        expo = jnp.exp2((score - jnp.concatenate([peak] * (keys // 128), axis=1)) * SCALE)
        added = expo[:, :128]
        for n in range(1, keys // 128):
            added = added + expo[:, n * 128 : (n + 1) * 128]
        total[span] = total[span] * fade + added
        top[span] = peak
        faded = acc[span] * jnp.concatenate([fade] * (LATENT // 128), axis=1)
        acc[span] = faded + dot(expo.astype(BF16), block[:LATENT], ((1,), (1,)))

    def attend(i, carry):
        for n, before in enumerate(befores):
            pl.when(i == n)(before)
        slots = pick([u[0] for u in UNITS], i), pick([u[1] for u in UNITS], i)
        quad = 2 * pick([u[2] for u in UNITS], i)
        block = jnp.concatenate([kbuf[s, quad + n] for s in slots for n in range(2)], axis=1)
        spans = [slice(r * chunk, (r + 1) * chunk) for r in range(2)]
        scores = [dot(qbuf[span], block) for span in spans]
        for r in range(2):
            score = scores[r]
            own = (score[:, :rows].reshape(heads, half, rows) + tri[r][None]).reshape(chunk, rows)
            soft(spans[r], jnp.concatenate([own, score[:, rows:]], axis=1), block)

        @pl.when(i == 0)
        def _():
            tri[...] = jnp.zeros_like(tri)

        return carry

    lax.fori_loop(0, len(befores), attend, 0)
    from_x(4)
    w_near.wait_recv()
    w_diag.start()
    loads[3].wait()
    loads[4].wait()
    far_core(6, 3, 5, 4)

    def az(way, step, r):
        source = (NZ - step) % NZ if way == 0 else step
        target = (NZ - step - 1) % NZ if way == 0 else step + 1
        return send(
            abuf.at[source, r], abuf.at[target, r],
            az_send.at[way, step, r], az_recv.at[way, step, r], along_z(1 - 2 * way),
        )

    for r in range(2):
        span = slice(r * chunk, (r + 1) * chunk)
        block = jnp.concatenate(
            [kbuf[s, 2 + n] for u in UNITS[len(befores) :] for s in u[:2] for n in range(2)], axis=1
        )
        soft(span, dot(qbuf[span], block), block)
        for n in range(heads):
            mine = slice((r * heads + n) * half, (r * heads + n + 1) * half)
            own = slice(n * VDIM, (n + 1) * VDIM)
            wide = acc[mine]
            high = wide.astype(BF16)
            low = (wide - high.astype(F32)).astype(BF16)
            summed = dot(high, upv[:, own]) + dot(low, upv[:, own])
            weight = jnp.sum(total[mine], axis=1, keepdims=True)
            abuf[0, r, :, own] = (summed / weight).astype(BF16)
        az(0, 0, r).start()
        az(1, 0, r).start()

    w_core.wait_recv()
    w_diag.wait_recv()

    my_r = lax.rem(y_hi + x, 2)
    mine = pl.ds(pl.multiple_of(my_r * half + x * part, part), part)

    def scatter(slot, r, n):
        k = lax.rem(x + n, NX)
        owner_y = lax.rem(k + r, 2)
        other = lax.rem(owner_y + y_hi, 2)
        there = pl.ds(pl.multiple_of(r * half + k * part, part), part)
        place = n - 1 + NX * other if n > 0 else NX - 1
        return send(
            pbuf.at[slot, there], rsbuf.at[slot, place],
            rs_send.at[slot, r, n], rs_recv.at[slot, place], (ctx, owner_y * NX + k),
        )

    def project(slots, r):
        made = jnp.concatenate([abuf[slot, r] for slot in slots], axis=0)
        made = dot(made, wbuf[...].reshape(NQ * cols, depth), ((1,), (1,))).astype(BF16)
        for n, slot in enumerate(slots):
            pbuf[slot, r * half : (r + 1) * half] = made[n * half : (n + 1) * half]
        for slot in slots:
            pl.when(my_r != r)(scatter(slot, r, 0).start)
            for n in range(1, NX):
                scatter(slot, r, n).start()

    def home(slot):
        return send(
            red.at[slot], obuf.at[mine], t_send.at[slot], t_recv.at[head],
            (lax.rem(z + slot, NZ) * NQ + q, z),
        )

    def reduce(slot):
        value = pbuf[slot, mine].astype(F32)
        for n in range(NH - 1):
            send(
                red.at[slot], rsbuf.at[slot, n],
                rs_send.at[slot, 0, 0], rs_recv.at[slot, n], to_core,
            ).wait_recv()
            value = value + rsbuf[slot, n].astype(F32)
        red[slot] = value.astype(BF16)
        if slot > 0:
            home(slot).start()
        else:
            pl.when(z != head)(home(0).start)

            @pl.when(z == head)
            def _():
                obuf[mine] = red[0]

    for r in range(2):
        project((0,), r)
    for step in range(1, last):
        for r in range(2):
            for way in range(2):
                az(way, step - 1, r).wait_recv()
            for way in range(2):
                if step < last - 1 or way == r:
                    az(way, step, r).start()
            project(slots_of(step), r)
        for slot in slots_of(step - 1):
            reduce(slot)
    for r in range(2):
        az(r, last - 1, r).wait_recv()
        project((last,), r)
    for slot in slots_of(last - 1):
        reduce(slot)
    reduce(last)

    for n in range(NH):
        there = pl.ds((n // NX + n) % 2 * half + n % NX * part, part)
        arrival = send(red.at[0], obuf.at[there], t_send.at[0], t_recv.at[n], to_core)
        pl.when(jnp.logical_or(z != head, head != n))(arrival.wait_recv)
    out[...] = obuf[...]

    for step in range(last):
        for way, k in z_pieces(step):
            kz(way, step, k).wait_send()
        for way in range(2):
            for r in range(2):
                if step < last - 1 or way == r:
                    az(way, step, r).wait_send()
    for slot in range(NZ):
        kc(slot).wait_send()
        for n in range(2):
            ky(slot, n).wait_send()
            kx(slot, n).wait_send()
            kd(slot, n).wait_send()
        for r in range(2):
            pl.when(my_r != r)(scatter(slot, r, 0).wait_send)
            for n in range(1, NX):
                scatter(slot, r, n).wait_send()
        if slot > 0:
            home(slot).wait_send()
        else:
            pl.when(z != head)(home(0).wait_send)
    w_core.wait_send()
    w_near.wait_send()
    w_diag.wait_send()


def per_device(q_nope, q_rope, latent_keys, kv_gain, up_key, up_value, out_proj, block_order):
    rows = q_nope.shape[0]
    heads = up_key.shape[1] // NOPE
    depth, cols = out_proj.shape
    wide = NQ * cols
    part = rows // NH
    dma = pltpu.SemaphoreType.DMA
    vmem = pl.BlockSpec(memory_space=pltpu.VMEM)
    hbm = pl.BlockSpec(memory_space=pl.ANY)
    return pl.pallas_call(
        kernel,
        out_shape=jax.ShapeDtypeStruct((rows, wide), BF16),
        in_specs=[pl.BlockSpec(memory_space=pltpu.SMEM), vmem, vmem] + [hbm] * 5,
        out_specs=vmem,
        scratch_shapes=[
            pltpu.VMEM(q_nope.shape, BF16),
            pltpu.VMEM(q_rope.shape, BF16),
            pltpu.VMEM(up_key.shape, BF16),
            pltpu.VMEM(up_value.shape, BF16),
            pltpu.VMEM((NQ, cols, depth), BF16),
            pltpu.VMEM((NZ, NQ, WIDTH, rows), BF16),
            pltpu.VMEM((heads * rows, WIDTH), BF16),
            pltpu.VMEM((heads * rows, LATENT), F32),
            pltpu.VMEM((heads * rows, 128), F32),
            pltpu.VMEM((heads * rows, 128), F32),
            pltpu.VMEM((2, rows // 2, rows), F32),
            pltpu.VMEM((NZ, 2, rows // 2, heads * VDIM), BF16),
            pltpu.VMEM((NZ, rows, wide), BF16),
            pltpu.VMEM((NZ, NH - 1, part, wide), BF16),
            pltpu.VMEM((NZ, part, wide), BF16),
            pltpu.VMEM((rows, wide), BF16),
            dma((5,)),
            dma((2, NZ // 2, 3)), dma((2, NZ // 2, 3)),
            dma((NZ,)), dma((NZ,)),
            dma((2, NZ)), dma((2, NZ)),
            dma((2, NZ)), dma((2, NZ)),
            dma((2, NZ)), dma((2, NZ)),
            dma((3,)), dma((3,)),
            dma((2, NZ // 2, 2)), dma((2, NZ // 2, 2)),
            dma((NZ, 2, NX)), dma((NZ, NH - 1)),
            dma((NZ,)), dma((NH,)),
        ],
        compiler_params=pltpu.CompilerParams(
            collective_id=0, has_side_effects=True, vmem_limit_bytes=56 * 1024 * 1024
        ),
    )(
        block_order, kv_gain.reshape(LATENT // 128, 128), latent_keys.T,
        q_nope, q_rope, up_key, up_value, out_proj.T,
    )


def solution(mesh):
    return jax.shard_map(
        per_device,
        mesh=mesh,
        in_specs=(
            P("ctx", "head"),
            P("ctx", "head"),
            P("ctx", None),
            P(),
            P(None, "head"),
            P(None, "head"),
            P("head", "ctx"),
            P(),
        ),
        out_specs=P("ctx", "head"),
        check_vma=False,
    )
```

```python
import math

import jax
import jax.numpy as jnp
from jax import lax
from jax.experimental import pallas as pl
from jax.experimental.pallas import tpu as pltpu
from jax.sharding import PartitionSpec as P

NOPE = 128
ROPE = 64
VDIM = 128
LATENT = 512
CARRIED = LATENT + ROPE
BLOCKS = 64
WIDTH = CARRIED + BLOCKS
NZ = 8
NQ = 4
NX = 4
NH = 8
HIDDEN = -1e30
SCALE = math.log2(math.e) / (NOPE + ROPE) ** 0.5
MESH = pl.DeviceIdType.MESH
F32 = jnp.float32
BF16 = jnp.bfloat16

HALF_WIDTH = CARRIED // 2
Y_PIECES = ((0, 192), (192, 96))
X_PIECES = ((0, 144), (144, 144))
UNITS = (
    ((0, 0), (0, 2)),
    ((2, 0), (6, 0)),
    ((1, 0), (7, 0)),
    ((3, 0), (5, 0)),
    ((2, 2), (6, 2)),
    ((1, 2), (7, 2)),
    ((3, 2), (5, 2)),
    ((4, 0), (4, 2)),
)


def dot(a, b, dims=((1,), (0,))):
    return lax.dot_general(a, b, (dims, ((), ())), preferred_element_type=F32)


def slots_of(step):
    if step == 0:
        return (0,)
    if step == NZ // 2:
        return (step,)
    return (step, NZ - step)


def pick(table, i):
    value = jnp.int32(table[0])
    for n in range(1, len(table)):
        value = jnp.where(i == n, table[n], value)
    return value


def kernel(
    order, gain, latent, qn_hbm, qr_hbm, upk_hbm, upv_hbm, w_hbm, out,
    qn, qr, upk, upv, wbuf, kbuf, qbuf, acc, top, total, tri, abuf, pbuf, rsbuf, red, obuf,
    load_sem, kz_send, kz_recv, kc_send, kc_recv, ky_send, ky_recv, kx_send, kx_recv,
    kd_send, kd_recv, w_send, w_recv, az_send, az_recv, rs_send, rs_recv, t_send, t_recv,
):
    rows = latent.shape[1]
    half = rows // 2
    heads = upk.shape[1] // NOPE
    cols, depth = w_hbm.shape
    part = rows // NH
    last = NZ // 2
    ctx = lax.axis_index("ctx")
    head = lax.axis_index("head")
    z, q = lax.div(ctx, NQ), lax.rem(ctx, NQ)
    y_lo, core = lax.div(q, 2), lax.rem(q, 2)
    y_hi, x = lax.div(head, NX), lax.rem(head, NX)
    x_odd = lax.rem(x, 2)
    q_core = q + 1 - 2 * core
    q_y = lax.rem(q + 2, NQ)
    q_diag = q_y + 1 - 2 * core
    quads = (q, q_core, q_y, q_diag)

    def along_z(step):
        return lax.rem(z + step + NZ, NZ) * NQ + q, head

    def along_x(step):
        return ctx, y_hi * NX + lax.rem(x + step + NX, NX)

    to_core = (z * NQ + q_core, head)
    to_near = (z * NQ + q_y, head)
    to_far = (z * NQ + q_y, lax.rem(y_hi + 1, 2) * NX + x)

    def send(src, dst, send_sem, recv_sem, device):
        return pltpu.make_async_remote_copy(
            src_ref=src, dst_ref=dst, send_sem=send_sem, recv_sem=recv_sem,
            device_id=device, device_id_type=MESH,
        )

    loads = [
        pltpu.make_async_copy(src, dst, load_sem.at[n])
        for n, (src, dst) in enumerate(
            ((qn_hbm, qn), (upk_hbm, upk), (qr_hbm, qr), (upv_hbm, upv), (w_hbm, wbuf.at[q]))
        )
    ]
    for load in loads:
        load.start()

    sources = [along_z(1), along_z(-1), along_z(2), along_z(-2), to_core, to_near, to_far]
    sources += [(ctx, lax.rem(head + n, NH)) for n in range(1, NH)]
    barrier = pltpu.get_barrier_semaphore()
    for device in sources:
        pl.semaphore_signal(barrier, inc=1, device_id=device, device_id_type=MESH)
    for n in range(NH):
        device = (head * NQ + q, n)

        @pl.when(jnp.logical_or(z != head, head != n))
        def _():
            pl.semaphore_signal(barrier, inc=1, device_id=device, device_id_type=MESH)

    plain = latent[:LATENT].astype(F32)
    inverse = lax.rsqrt(jnp.mean(plain * plain, axis=0, keepdims=True) + 1e-06)
    for n in range(LATENT // 128):
        span = slice(n * 128, (n + 1) * 128)
        column = jnp.broadcast_to(gain[n : n + 1], (128, 128)).T
        kbuf[0, 0, span] = (plain[span] * inverse * column).astype(BF16)
    kbuf[0, 0, LATENT:CARRIED] = latent[LATENT:]

    def kept(odd, first, size):
        return pl.ds(pl.multiple_of(odd * HALF_WIDTH + first, 16), size)

    def kz(way, step):
        size = HALF_WIDTH if step < last else HALF_WIDTH // 2
        span = kept(x_odd, way * size if step == last else 0, size)
        hops, gone = (step, 0) if step < 3 else (step - 2, 2)
        source = (NZ - gone) % NZ if way == 0 else gone
        target = NZ - step if way == 0 else step
        return send(
            kbuf.at[source, 0, span], kbuf.at[target, 0, span],
            kz_send.at[way, step - 1], kz_recv.at[way, step - 1], along_z(hops * (1 - 2 * way)),
        )

    def kc(slot, n):
        span = kept(x_odd if n == 0 else 1 - x_odd, 0, HALF_WIDTH)
        return send(
            kbuf.at[slot, 0, span], kbuf.at[slot, 1, span],
            kc_send.at[n, slot], kc_recv.at[n, slot], to_core,
        )

    def ky(slot, n):
        span = kept(x_odd, *Y_PIECES[n])
        return send(
            kbuf.at[slot, 0, span], kbuf.at[slot, 2, span],
            ky_send.at[n, slot], ky_recv.at[n, slot], (to_far, to_near)[n],
        )

    def kx(quad, slot, n, coming=False):
        span = kept(1 - x_odd if coming else x_odd, *X_PIECES[n])
        return send(
            kbuf.at[slot, quad, span], kbuf.at[slot, quad, span],
            kx_send.at[quad // 2, n, slot], kx_recv.at[quad // 2, n, slot], along_x(1 - 2 * n),
        )

    def kd(slot, n):
        span = kept(x_odd if n == 0 else 1 - x_odd, 0, HALF_WIDTH)
        return send(
            kbuf.at[slot, 2, span], kbuf.at[slot, 3, span],
            kd_send.at[n, slot], kd_recv.at[n, slot], to_core,
        )

    w_core = send(w_hbm, wbuf.at[q], w_send.at[0], w_recv.at[0], to_core)
    w_near = send(w_hbm, wbuf.at[q], w_send.at[1], w_recv.at[1], to_near)
    w_diag = send(wbuf.at[q_y], wbuf.at[q_y], w_send.at[2], w_recv.at[2], to_core)

    def share(step):
        for slot in slots_of(step):
            for n in range(2):
                if step > 0:
                    kx(0, slot, n).start()
                ky(slot, n).start()
            kc(slot, 0).start()
            if step == 0:
                kc(slot, 1).start()

    def from_z(step):
        for way in range(2):
            kz(way, step).wait_recv()
        if step == 2:
            for way in range(2):
                kz(way, 3).start()
                kz(way, 4).start()
        share(step)

    def from_own_x(step):
        for slot in slots_of(step):
            for n in range(2):
                kx(0, slot, n, True).wait_recv()
            kc(slot, 1).start()

    def from_y(step):
        for slot in slots_of(step):
            for n in range(2):
                ky(slot, n).wait_recv()
            for n in range(2):
                kx(2, slot, n).start()
            kd(slot, 0).start()

    def from_x(step):
        for slot in slots_of(step):
            for n in range(2):
                kx(2, slot, n, True).wait_recv()
            kd(slot, 1).start()

    def near_core(step):
        for slot in slots_of(step):
            kc(slot, 0).wait_recv()
            kc(slot, 1).wait_recv()

    def far_core(step):
        for slot in slots_of(step):
            kd(slot, 0).wait_recv()
            kd(slot, 1).wait_recv()

    pl.semaphore_wait(barrier, len(sources) + NH - jnp.where(z == head, 1, 0))
    for step in (2, 1):
        for way in range(2):
            kz(way, step).start()
    share(0)
    w_near.start()
    w_core.start()

    which = lax.broadcasted_iota(jnp.int32, (BLOCKS, rows), 0)
    first_half = lax.broadcasted_iota(jnp.int32, (BLOCKS, rows), 1) < half

    def mark(slot, carry):
        from_z = lax.rem(z + slot, NZ) * NQ
        for n, quad in enumerate(quads):
            there = 2 * (from_z + quad)
            owner = jnp.where(first_half, order[there], order[there + 1])
            kbuf[slot, n, CARRIED:] = jnp.where(which == owner, 1.0, 0.0).astype(BF16)
        return carry

    lax.fori_loop(0, NZ, mark, 0)
    lane = lax.broadcasted_iota(jnp.int32, (half, BLOCKS), 1)
    for r in range(2):
        row = lax.broadcasted_iota(jnp.int32, (half, rows), 0)
        key = lax.broadcasted_iota(jnp.int32, (half, rows), 1) - r * half
        tri[r] = jnp.where(jnp.logical_and(key > row, key < half), HIDDEN, 0.0)
    acc[...] = jnp.zeros_like(acc)
    total[...] = jnp.zeros_like(total)
    top[...] = jnp.full_like(top, HIDDEN)

    loads[0].wait()
    loads[1].wait()
    loads[2].wait()
    for n in range(heads):
        own = slice(n * NOPE, (n + 1) * NOPE)
        turned = dot(qn[:, own], upk[:, own], ((1,), (1,))).astype(BF16)
        rope = qr[:, n * ROPE : (n + 1) * ROPE]
        for r in range(2):
            span = slice((r * heads + n) * half, (r * heads + n + 1) * half)
            mine = slice(r * half, (r + 1) * half)
            later = jnp.where(lane > order[2 * ctx + r], HIDDEN, 0.0).astype(BF16)
            qbuf[span, :LATENT] = turned[mine]
            qbuf[span, LATENT:] = jnp.concatenate([rope[mine], later], axis=1)

    from_y(0)
    from_z(2)
    from_x(0)
    from_z(1)

    def before_0():
        near_core(0)
        far_core(0)

    def before_1():
        from_own_x(2)
        from_z(3)
        from_y(2)
        near_core(2)

    def before_2():
        from_own_x(1)
        from_z(4)
        from_y(1)
        near_core(1)

    def before_3():
        from_own_x(3)
        from_y(3)
        near_core(3)

    def before_4():
        from_x(2)
        from_y(4)
        from_own_x(4)
        far_core(2)

    def before_5():
        from_x(1)
        w_near.wait_recv()
        w_diag.start()
        far_core(1)

    befores = (before_0, before_1, before_2, before_3, before_4, before_5)
    chunk = heads * half

    def soft(span, score, block):
        keys = score.shape[1]
        before = top[span]
        peak = jnp.maximum(before, jnp.max(score, axis=1, keepdims=True))
        fade = jnp.exp2((before - peak) * SCALE)
        expo = jnp.exp2((score - jnp.concatenate([peak] * (keys // 128), axis=1)) * SCALE)
        added = expo[:, :128]
        for n in range(1, keys // 128):
            added = added + expo[:, n * 128 : (n + 1) * 128]
        total[span] = total[span] * fade + added
        top[span] = peak
        faded = acc[span] * jnp.concatenate([fade] * (LATENT // 128), axis=1)
        acc[span] = faded + dot(expo.astype(BF16), block[:LATENT], ((1,), (1,)))

    def attend(i, carry):
        for n, before in enumerate(befores):
            pl.when(i == n)(before)
        pairs = [[pick([u[m][n] for u in UNITS], i) for n in range(2)] for m in range(2)]
        block = jnp.concatenate([kbuf[s, quad + n] for s, quad in pairs for n in range(2)], axis=1)
        spans = [slice(r * chunk, (r + 1) * chunk) for r in range(2)]
        scores = [dot(qbuf[span], block) for span in spans]
        for r in range(2):
            score = scores[r]
            own = (score[:, :rows].reshape(heads, half, rows) + tri[r][None]).reshape(chunk, rows)
            soft(spans[r], jnp.concatenate([own, score[:, rows:]], axis=1), block)

        @pl.when(i == 0)
        def _():
            tri[...] = jnp.zeros_like(tri)

        return carry

    lax.fori_loop(0, len(befores), attend, 0)
    from_x(3)
    from_x(4)
    loads[3].wait()
    loads[4].wait()
    near_core(4)
    far_core(3)
    far_core(4)

    def az(way, step, r):
        source = (NZ - step) % NZ if way == 0 else step
        target = (NZ - step - 1) % NZ if way == 0 else step + 1
        return send(
            abuf.at[source, r], abuf.at[target, r],
            az_send.at[way, step, r], az_recv.at[way, step, r], along_z(1 - 2 * way),
        )

    for r in range(2):
        span = slice(r * chunk, (r + 1) * chunk)
        block = jnp.concatenate(
            [kbuf[s, quad + n] for u in UNITS[len(befores) :] for s, quad in u for n in range(2)],
            axis=1,
        )
        soft(span, dot(qbuf[span], block), block)
        for n in range(heads):
            mine = slice((r * heads + n) * half, (r * heads + n + 1) * half)
            own = slice(n * VDIM, (n + 1) * VDIM)
            wide = acc[mine]
            high = wide.astype(BF16)
            low = (wide - high.astype(F32)).astype(BF16)
            summed = dot(high, upv[:, own]) + dot(low, upv[:, own])
            weight = jnp.sum(total[mine], axis=1, keepdims=True)
            abuf[0, r, :, own] = (summed / weight).astype(BF16)
        az(0, 0, r).start()
        az(1, 0, r).start()

    w_core.wait_recv()
    w_diag.wait_recv()

    my_r = lax.rem(y_hi + x, 2)
    mine = pl.ds(pl.multiple_of(my_r * half + x * part, part), part)

    def scatter(slot, r, n):
        k = lax.rem(x + n, NX)
        owner_y = lax.rem(k + r, 2)
        other = lax.rem(owner_y + y_hi, 2)
        there = pl.ds(pl.multiple_of(r * half + k * part, part), part)
        place = n - 1 + NX * other if n > 0 else NX - 1
        return send(
            pbuf.at[slot, there], rsbuf.at[slot, place],
            rs_send.at[slot, r, n], rs_recv.at[slot, place], (ctx, owner_y * NX + k),
        )

    def project(slots, r):
        made = jnp.concatenate([abuf[slot, r] for slot in slots], axis=0)
        made = dot(made, wbuf[...].reshape(NQ * cols, depth), ((1,), (1,))).astype(BF16)
        for n, slot in enumerate(slots):
            pbuf[slot, r * half : (r + 1) * half] = made[n * half : (n + 1) * half]
        for slot in slots:
            pl.when(my_r != r)(scatter(slot, r, 0).start)
            for n in range(1, NX):
                scatter(slot, r, n).start()

    def home(slot):
        return send(
            red.at[slot], obuf.at[mine], t_send.at[slot], t_recv.at[head],
            (lax.rem(z + slot, NZ) * NQ + q, z),
        )

    def reduce(slot):
        value = pbuf[slot, mine].astype(F32)
        for n in range(NH - 1):
            send(
                red.at[slot], rsbuf.at[slot, n],
                rs_send.at[slot, 0, 0], rs_recv.at[slot, n], to_core,
            ).wait_recv()
            value = value + rsbuf[slot, n].astype(F32)
        red[slot] = value.astype(BF16)
        if slot > 0:
            home(slot).start()
        else:
            pl.when(z != head)(home(0).start)

            @pl.when(z == head)
            def _():
                obuf[mine] = red[0]

    for r in range(2):
        project((0,), r)
    for step in range(1, last):
        for r in range(2):
            for way in range(2):
                az(way, step - 1, r).wait_recv()
            for way in range(2):
                if step < last - 1 or way == r:
                    az(way, step, r).start()
            project(slots_of(step), r)
        for slot in slots_of(step - 1):
            reduce(slot)
    for r in range(2):
        az(r, last - 1, r).wait_recv()
        project((last,), r)
    for slot in slots_of(last - 1):
        reduce(slot)
    reduce(last)

    for n in range(NH):
        there = pl.ds((n // NX + n) % 2 * half + n % NX * part, part)
        arrival = send(red.at[0], obuf.at[there], t_send.at[0], t_recv.at[n], to_core)
        pl.when(jnp.logical_or(z != head, head != n))(arrival.wait_recv)
    out[...] = obuf[...]

    for step in range(last):
        for way in range(2):
            kz(way, step + 1).wait_send()
            for r in range(2):
                if step < last - 1 or way == r:
                    az(way, step, r).wait_send()
    for slot in range(NZ):
        for n in range(2):
            kc(slot, n).wait_send()
            ky(slot, n).wait_send()
            kx(2, slot, n).wait_send()
            if slot > 0:
                kx(0, slot, n).wait_send()
            kd(slot, n).wait_send()
        for r in range(2):
            pl.when(my_r != r)(scatter(slot, r, 0).wait_send)
            for n in range(1, NX):
                scatter(slot, r, n).wait_send()
        if slot > 0:
            home(slot).wait_send()
        else:
            pl.when(z != head)(home(0).wait_send)
    w_core.wait_send()
    w_near.wait_send()
    w_diag.wait_send()


def per_device(q_nope, q_rope, latent_keys, kv_gain, up_key, up_value, out_proj, block_order):
    rows = q_nope.shape[0]
    heads = up_key.shape[1] // NOPE
    depth, cols = out_proj.shape
    wide = NQ * cols
    part = rows // NH
    dma = pltpu.SemaphoreType.DMA
    vmem = pl.BlockSpec(memory_space=pltpu.VMEM)
    hbm = pl.BlockSpec(memory_space=pl.ANY)
    return pl.pallas_call(
        kernel,
        out_shape=jax.ShapeDtypeStruct((rows, wide), BF16),
        in_specs=[pl.BlockSpec(memory_space=pltpu.SMEM), vmem, vmem] + [hbm] * 5,
        out_specs=vmem,
        scratch_shapes=[
            pltpu.VMEM(q_nope.shape, BF16),
            pltpu.VMEM(q_rope.shape, BF16),
            pltpu.VMEM(up_key.shape, BF16),
            pltpu.VMEM(up_value.shape, BF16),
            pltpu.VMEM((NQ, cols, depth), BF16),
            pltpu.VMEM((NZ, NQ, WIDTH, rows), BF16),
            pltpu.VMEM((heads * rows, WIDTH), BF16),
            pltpu.VMEM((heads * rows, LATENT), F32),
            pltpu.VMEM((heads * rows, 128), F32),
            pltpu.VMEM((heads * rows, 128), F32),
            pltpu.VMEM((2, rows // 2, rows), F32),
            pltpu.VMEM((NZ, 2, rows // 2, heads * VDIM), BF16),
            pltpu.VMEM((NZ, rows, wide), BF16),
            pltpu.VMEM((NZ, NH - 1, part, wide), BF16),
            pltpu.VMEM((NZ, part, wide), BF16),
            pltpu.VMEM((rows, wide), BF16),
            dma((5,)),
            dma((2, NZ // 2)), dma((2, NZ // 2)),
            dma((2, NZ)), dma((2, NZ)),
            dma((2, NZ)), dma((2, NZ)),
            dma((2, 2, NZ)), dma((2, 2, NZ)),
            dma((2, NZ)), dma((2, NZ)),
            dma((3,)), dma((3,)),
            dma((2, NZ // 2, 2)), dma((2, NZ // 2, 2)),
            dma((NZ, 2, NX)), dma((NZ, NH - 1)),
            dma((NZ,)), dma((NH,)),
        ],
        compiler_params=pltpu.CompilerParams(
            collective_id=0, has_side_effects=True, vmem_limit_bytes=56 * 1024 * 1024
        ),
    )(
        block_order, kv_gain.reshape(LATENT // 128, 128), latent_keys.T,
        q_nope, q_rope, up_key, up_value, out_proj.T,
    )


def solution(mesh):
    return jax.shard_map(
        per_device,
        mesh=mesh,
        in_specs=(
            P("ctx", "head"),
            P("ctx", "head"),
            P("ctx", None),
            P(),
            P(None, "head"),
            P(None, "head"),
            P("head", "ctx"),
            P(),
        ),
        out_specs=P("ctx", "head"),
        check_vma=False,
    )
```

```python
import math

import jax
import jax.numpy as jnp
from jax import lax
from jax.experimental import pallas as pl
from jax.experimental.pallas import tpu as pltpu
from jax.sharding import PartitionSpec as P

NOPE = 128
ROPE = 64
VDIM = 128
LATENT = 512
CARRIED = LATENT + ROPE
BLOCKS = 64
WIDTH = CARRIED + BLOCKS
NZ = 8
NQ = 4
NX = 4
NH = 8
HIDDEN = -1e30
SCALE = math.log2(math.e) / (NOPE + ROPE) ** 0.5
MESH = pl.DeviceIdType.MESH
F32 = jnp.float32
BF16 = jnp.bfloat16

HALF_WIDTH = CARRIED // 2
Y_PIECES = ((0, 192), (192, 96))
X_PIECES = ((0, 144), (144, 144))
UNITS = (
    ((0, 0), (0, 2)),
    ((2, 0), (6, 0)),
    ((1, 0), (7, 0)),
    ((3, 0), (5, 0)),
    ((2, 2), (6, 2)),
    ((1, 2), (7, 2)),
    ((3, 2), (5, 2)),
    ((4, 0), (4, 2)),
)


def dot(a, b, dims=((1,), (0,))):
    return lax.dot_general(a, b, (dims, ((), ())), preferred_element_type=F32)


def slots_of(step):
    if step == 0:
        return (0,)
    if step == NZ // 2:
        return (step,)
    return (step, NZ - step)


def pick(table, i):
    value = jnp.int32(table[0])
    for n in range(1, len(table)):
        value = jnp.where(i == n, table[n], value)
    return value


def kernel(
    order, gain, latent, qn_hbm, qr_hbm, upk_hbm, upv_hbm, w_hbm, out,
    qn, qr, upk, upv, wbuf, kbuf, qbuf, acc, top, total, tri, abuf, pbuf, rsbuf, red, obuf,
    load_sem, kz_send, kz_recv, kn_send, kn_recv, kc_send, kc_recv, ky_send, ky_recv, kx_send, kx_recv,
    kd_send, kd_recv, w_send, w_recv, az_send, az_recv, rs_send, rs_recv, t_send, t_recv,
):
    rows = latent.shape[1]
    half = rows // 2
    heads = upk.shape[1] // NOPE
    cols, depth = w_hbm.shape
    part = rows // NH
    last = NZ // 2
    ctx = lax.axis_index("ctx")
    head = lax.axis_index("head")
    z, q = lax.div(ctx, NQ), lax.rem(ctx, NQ)
    y_lo, core = lax.div(q, 2), lax.rem(q, 2)
    y_hi, x = lax.div(head, NX), lax.rem(head, NX)
    x_odd = lax.rem(x, 2)
    q_core = q + 1 - 2 * core
    q_y = lax.rem(q + 2, NQ)
    q_diag = q_y + 1 - 2 * core
    quads = (q, q_core, q_y, q_diag)

    def along_z(step):
        return lax.rem(z + step + NZ, NZ) * NQ + q, head

    def along_x(step):
        return ctx, y_hi * NX + lax.rem(x + step + NX, NX)

    to_core = (z * NQ + q_core, head)
    to_near = (z * NQ + q_y, head)
    to_far = (z * NQ + q_y, lax.rem(y_hi + 1, 2) * NX + x)

    def send(src, dst, send_sem, recv_sem, device):
        return pltpu.make_async_remote_copy(
            src_ref=src, dst_ref=dst, send_sem=send_sem, recv_sem=recv_sem,
            device_id=device, device_id_type=MESH,
        )

    loads = [
        pltpu.make_async_copy(src, dst, load_sem.at[n])
        for n, (src, dst) in enumerate(
            ((qn_hbm, qn), (upk_hbm, upk), (qr_hbm, qr), (upv_hbm, upv), (w_hbm, wbuf.at[q]))
        )
    ]
    for load in loads:
        load.start()

    sources = [along_z(1), along_z(-1), along_z(2), along_z(-2), to_core, to_near, to_far]
    sources += [(ctx, lax.rem(head + n, NH)) for n in range(1, NH)]
    barrier = pltpu.get_barrier_semaphore()
    for device in sources:
        pl.semaphore_signal(barrier, inc=1, device_id=device, device_id_type=MESH)
    for n in range(NH):
        device = (head * NQ + q, n)

        @pl.when(jnp.logical_or(z != head, head != n))
        def _():
            pl.semaphore_signal(barrier, inc=1, device_id=device, device_id_type=MESH)

    plain = latent[:LATENT].astype(F32)
    inverse = lax.rsqrt(jnp.mean(plain * plain, axis=0, keepdims=True) + 1e-06)
    for n in range(LATENT // 128):
        span = slice(n * 128, (n + 1) * 128)
        column = jnp.broadcast_to(gain[n : n + 1], (128, 128)).T
        kbuf[0, 0, span] = (plain[span] * inverse * column).astype(BF16)
    kbuf[0, 0, LATENT:CARRIED] = latent[LATENT:]

    def kept(odd, first, size):
        return pl.ds(pl.multiple_of(odd * HALF_WIDTH + first, 16), size)

    def kz(way, step):
        size = HALF_WIDTH if step < last else HALF_WIDTH // 2
        span = kept(x_odd, way * size if step == last else 0, size)
        hops, gone = (step, 0) if step < 3 else (step - 2, 2)
        source = (NZ - gone) % NZ if way == 0 else gone
        target = NZ - step if way == 0 else step
        return send(
            kbuf.at[source, 0, span], kbuf.at[target, 0, span],
            kz_send.at[way, step - 1], kz_recv.at[way, step - 1], along_z(hops * (1 - 2 * way)),
        )

    def kn(way):
        span = kept(1 - x_odd, 0, HALF_WIDTH)
        target = NZ - 1 if way == 0 else 1
        return send(
            kbuf.at[0, 0, span], kbuf.at[target, 0, span],
            kn_send.at[way], kn_recv.at[way], along_z(1 - 2 * way),
        )

    def kc(slot, n):
        span = kept(x_odd if n == 0 else 1 - x_odd, 0, HALF_WIDTH)
        return send(
            kbuf.at[slot, 0, span], kbuf.at[slot, 1, span],
            kc_send.at[n, slot], kc_recv.at[n, slot], to_core,
        )

    def ky(slot, n):
        span = kept(x_odd, *Y_PIECES[n])
        return send(
            kbuf.at[slot, 0, span], kbuf.at[slot, 2, span],
            ky_send.at[n, slot], ky_recv.at[n, slot], (to_far, to_near)[n],
        )

    def kx(quad, slot, n, coming=False):
        span = kept(1 - x_odd if coming else x_odd, *X_PIECES[n])
        return send(
            kbuf.at[slot, quad, span], kbuf.at[slot, quad, span],
            kx_send.at[quad // 2, n, slot], kx_recv.at[quad // 2, n, slot], along_x(1 - 2 * n),
        )

    def kd(slot, n):
        span = kept(x_odd if n == 0 else 1 - x_odd, 0, HALF_WIDTH)
        return send(
            kbuf.at[slot, 2, span], kbuf.at[slot, 3, span],
            kd_send.at[n, slot], kd_recv.at[n, slot], to_core,
        )

    w_core = send(w_hbm, wbuf.at[q], w_send.at[0], w_recv.at[0], to_core)
    w_near = send(w_hbm, wbuf.at[q], w_send.at[1], w_recv.at[1], to_near)
    w_diag = send(wbuf.at[q_y], wbuf.at[q_y], w_send.at[2], w_recv.at[2], to_core)

    def share(step):
        for slot in slots_of(step):
            for n in range(2):
                if step > 1:
                    kx(0, slot, n).start()
                ky(slot, n).start()
            kc(slot, 0).start()
            if step == 0:
                kc(slot, 1).start()

    def from_z(step):
        for way in range(2):
            kz(way, step).wait_recv()
        if step == 2:
            for way in range(2):
                kz(way, 3).start()
                kz(way, 4).start()
            for way in range(2):
                kn(way).start()
        share(step)

    def from_own_x(step):
        for slot in slots_of(step):
            if step == 1:
                kn(0 if slot > 1 else 1).wait_recv()
            else:
                for n in range(2):
                    kx(0, slot, n, True).wait_recv()
            kc(slot, 1).start()

    def from_y(step):
        for slot in slots_of(step):
            for n in range(2):
                ky(slot, n).wait_recv()
            for n in range(2):
                kx(2, slot, n).start()
            kd(slot, 0).start()

    def from_x(step):
        for slot in slots_of(step):
            for n in range(2):
                kx(2, slot, n, True).wait_recv()
            kd(slot, 1).start()

    def near_core(step):
        for slot in slots_of(step):
            kc(slot, 0).wait_recv()
            kc(slot, 1).wait_recv()

    def far_core(step):
        for slot in slots_of(step):
            kd(slot, 0).wait_recv()
            kd(slot, 1).wait_recv()

    pl.semaphore_wait(barrier, len(sources) + NH - jnp.where(z == head, 1, 0))
    for step in (2, 1):
        for way in range(2):
            kz(way, step).start()
    share(0)
    w_near.start()
    w_core.start()

    which = lax.broadcasted_iota(jnp.int32, (BLOCKS, rows), 0)
    first_half = lax.broadcasted_iota(jnp.int32, (BLOCKS, rows), 1) < half

    def mark(slot, carry):
        from_z = lax.rem(z + slot, NZ) * NQ
        for n, quad in enumerate(quads):
            there = 2 * (from_z + quad)
            owner = jnp.where(first_half, order[there], order[there + 1])
            kbuf[slot, n, CARRIED:] = jnp.where(which == owner, 1.0, 0.0).astype(BF16)
        return carry

    lax.fori_loop(0, NZ, mark, 0)
    lane = lax.broadcasted_iota(jnp.int32, (half, BLOCKS), 1)
    for r in range(2):
        row = lax.broadcasted_iota(jnp.int32, (half, rows), 0)
        key = lax.broadcasted_iota(jnp.int32, (half, rows), 1) - r * half
        tri[r] = jnp.where(jnp.logical_and(key > row, key < half), HIDDEN, 0.0)
    acc[...] = jnp.zeros_like(acc)
    total[...] = jnp.zeros_like(total)
    top[...] = jnp.full_like(top, HIDDEN)

    loads[0].wait()
    loads[1].wait()
    loads[2].wait()
    for n in range(heads):
        own = slice(n * NOPE, (n + 1) * NOPE)
        turned = dot(qn[:, own], upk[:, own], ((1,), (1,))).astype(BF16)
        rope = qr[:, n * ROPE : (n + 1) * ROPE]
        for r in range(2):
            span = slice((r * heads + n) * half, (r * heads + n + 1) * half)
            mine = slice(r * half, (r + 1) * half)
            later = jnp.where(lane > order[2 * ctx + r], HIDDEN, 0.0).astype(BF16)
            qbuf[span, :LATENT] = turned[mine]
            qbuf[span, LATENT:] = jnp.concatenate([rope[mine], later], axis=1)

    from_y(0)
    from_z(2)
    from_x(0)
    from_z(1)

    def before_0():
        near_core(0)
        far_core(0)

    def before_1():
        from_own_x(2)
        from_z(3)
        from_y(2)
        near_core(2)

    def before_2():
        from_z(4)
        from_own_x(1)
        from_y(1)
        from_own_x(3)
        near_core(1)

    def before_3():
        from_y(3)
        from_x(2)
        from_y(4)
        near_core(3)

    def before_4():
        from_own_x(4)
        from_x(1)
        far_core(2)

    def before_5():
        w_near.wait_recv()
        w_diag.start()
        from_x(3)
        from_x(4)
        far_core(1)

    befores = (before_0, before_1, before_2, before_3, before_4, before_5)
    chunk = heads * half

    def soft(span, score, block):
        keys = score.shape[1]
        before = top[span]
        peak = jnp.maximum(before, jnp.max(score, axis=1, keepdims=True))
        fade = jnp.exp2((before - peak) * SCALE)
        expo = jnp.exp2((score - jnp.concatenate([peak] * (keys // 128), axis=1)) * SCALE)
        added = expo[:, :128]
        for n in range(1, keys // 128):
            added = added + expo[:, n * 128 : (n + 1) * 128]
        total[span] = total[span] * fade + added
        top[span] = peak
        faded = acc[span] * jnp.concatenate([fade] * (LATENT // 128), axis=1)
        acc[span] = faded + dot(expo.astype(BF16), block[:LATENT], ((1,), (1,)))

    def attend(i, carry):
        for n, before in enumerate(befores):
            pl.when(i == n)(before)
        pairs = [[pick([u[m][n] for u in UNITS], i) for n in range(2)] for m in range(2)]
        block = jnp.concatenate([kbuf[s, quad + n] for s, quad in pairs for n in range(2)], axis=1)
        spans = [slice(r * chunk, (r + 1) * chunk) for r in range(2)]
        scores = [dot(qbuf[span], block) for span in spans]
        for r in range(2):
            score = scores[r]
            own = (score[:, :rows].reshape(heads, half, rows) + tri[r][None]).reshape(chunk, rows)
            soft(spans[r], jnp.concatenate([own, score[:, rows:]], axis=1), block)

        @pl.when(i == 0)
        def _():
            tri[...] = jnp.zeros_like(tri)

        return carry

    lax.fori_loop(0, len(befores), attend, 0)
    loads[3].wait()
    loads[4].wait()
    near_core(4)
    far_core(3)
    far_core(4)

    def az(way, step, r):
        source = (NZ - step) % NZ if way == 0 else step
        target = (NZ - step - 1) % NZ if way == 0 else step + 1
        src, dst = abuf.at[source, r], abuf.at[target, r]
        if step == last - 1:
            span = pl.ds(way * (half // 2), half // 2)
            src, dst = src.at[span], dst.at[span]
        return send(
            src, dst, az_send.at[way, step, r], az_recv.at[way, step, r], along_z(1 - 2 * way),
        )

    for r in range(2):
        span = slice(r * chunk, (r + 1) * chunk)
        block = jnp.concatenate(
            [kbuf[s, quad + n] for u in UNITS[len(befores) :] for s, quad in u for n in range(2)],
            axis=1,
        )
        soft(span, dot(qbuf[span], block), block)
        for n in range(heads):
            mine = slice((r * heads + n) * half, (r * heads + n + 1) * half)
            own = slice(n * VDIM, (n + 1) * VDIM)
            wide = acc[mine]
            high = wide.astype(BF16)
            low = (wide - high.astype(F32)).astype(BF16)
            summed = dot(high, upv[:, own]) + dot(low, upv[:, own])
            weight = jnp.sum(total[mine], axis=1, keepdims=True)
            abuf[0, r, :, own] = (summed / weight).astype(BF16)
        az(0, 0, r).start()
        az(1, 0, r).start()

    w_core.wait_recv()
    w_diag.wait_recv()

    my_r = lax.rem(y_hi + x, 2)
    mine = pl.ds(pl.multiple_of(my_r * half + x * part, part), part)

    def scatter(slot, r, n):
        k = lax.rem(x + n, NX)
        owner_y = lax.rem(k + r, 2)
        other = lax.rem(owner_y + y_hi, 2)
        there = pl.ds(pl.multiple_of(r * half + k * part, part), part)
        place = n - 1 + NX * other if n > 0 else NX - 1
        return send(
            pbuf.at[slot, there], rsbuf.at[slot, place],
            rs_send.at[slot, r, n], rs_recv.at[slot, place], (ctx, owner_y * NX + k),
        )

    def project(slots, r):
        made = jnp.concatenate([abuf[slot, r] for slot in slots], axis=0)
        made = dot(made, wbuf[...].reshape(NQ * cols, depth), ((1,), (1,))).astype(BF16)
        for n, slot in enumerate(slots):
            pbuf[slot, r * half : (r + 1) * half] = made[n * half : (n + 1) * half]
        for slot in slots:
            pl.when(my_r != r)(scatter(slot, r, 0).start)
            for n in range(1, NX):
                scatter(slot, r, n).start()

    def home(slot):
        return send(
            red.at[slot], obuf.at[mine], t_send.at[slot], t_recv.at[head],
            (lax.rem(z + slot, NZ) * NQ + q, z),
        )

    def reduce(slot):
        value = pbuf[slot, mine].astype(F32)
        for n in range(NH - 1):
            send(
                red.at[slot], rsbuf.at[slot, n],
                rs_send.at[slot, 0, 0], rs_recv.at[slot, n], to_core,
            ).wait_recv()
            value = value + rsbuf[slot, n].astype(F32)
        red[slot] = value.astype(BF16)

    def go_home(slot):
        if slot > 0:
            home(slot).start()
        else:
            pl.when(z != head)(home(0).start)

            @pl.when(z == head)
            def _():
                obuf[mine] = red[0]

    for r in range(2):
        project((0,), r)
    for step in range(1, last):
        for r in range(2):
            for way in range(2):
                az(way, step - 1, r).wait_recv()
            for way in range(2):
                az(way, step, r).start()
            project(slots_of(step), r)
        for slot in slots_of(step - 1):
            reduce(slot)
        if step == 1:
            go_home(0)
    for r in range(2):
        for way in range(2):
            az(way, last - 1, r).wait_recv()
        project((last,), r)
    for slot in slots_of(2) + slots_of(1):
        go_home(slot)
    for slot in slots_of(last - 1) + slots_of(last):
        reduce(slot)
        go_home(slot)

    for n in range(NH):
        there = pl.ds((n // NX + n) % 2 * half + n % NX * part, part)
        arrival = send(red.at[0], obuf.at[there], t_send.at[0], t_recv.at[n], to_core)
        pl.when(jnp.logical_or(z != head, head != n))(arrival.wait_recv)
    out[...] = obuf[...]

    for step in range(last):
        for way in range(2):
            kz(way, step + 1).wait_send()
            for r in range(2):
                az(way, step, r).wait_send()
    for slot in range(NZ):
        for n in range(2):
            kc(slot, n).wait_send()
            ky(slot, n).wait_send()
            kx(2, slot, n).wait_send()
            if slot not in slots_of(0) + slots_of(1):
                kx(0, slot, n).wait_send()
            kd(slot, n).wait_send()
        for r in range(2):
            pl.when(my_r != r)(scatter(slot, r, 0).wait_send)
            for n in range(1, NX):
                scatter(slot, r, n).wait_send()
        if slot > 0:
            home(slot).wait_send()
        else:
            pl.when(z != head)(home(0).wait_send)
    kn(0).wait_send()
    kn(1).wait_send()
    w_core.wait_send()
    w_near.wait_send()
    w_diag.wait_send()


def per_device(q_nope, q_rope, latent_keys, kv_gain, up_key, up_value, out_proj, block_order):
    rows = q_nope.shape[0]
    heads = up_key.shape[1] // NOPE
    depth, cols = out_proj.shape
    wide = NQ * cols
    part = rows // NH
    dma = pltpu.SemaphoreType.DMA
    vmem = pl.BlockSpec(memory_space=pltpu.VMEM)
    hbm = pl.BlockSpec(memory_space=pl.ANY)
    return pl.pallas_call(
        kernel,
        out_shape=jax.ShapeDtypeStruct((rows, wide), BF16),
        in_specs=[pl.BlockSpec(memory_space=pltpu.SMEM), vmem, vmem] + [hbm] * 5,
        out_specs=vmem,
        scratch_shapes=[
            pltpu.VMEM(q_nope.shape, BF16),
            pltpu.VMEM(q_rope.shape, BF16),
            pltpu.VMEM(up_key.shape, BF16),
            pltpu.VMEM(up_value.shape, BF16),
            pltpu.VMEM((NQ, cols, depth), BF16),
            pltpu.VMEM((NZ, NQ, WIDTH, rows), BF16),
            pltpu.VMEM((heads * rows, WIDTH), BF16),
            pltpu.VMEM((heads * rows, LATENT), F32),
            pltpu.VMEM((heads * rows, 128), F32),
            pltpu.VMEM((heads * rows, 128), F32),
            pltpu.VMEM((2, rows // 2, rows), F32),
            pltpu.VMEM((NZ, 2, rows // 2, heads * VDIM), BF16),
            pltpu.VMEM((NZ, rows, wide), BF16),
            pltpu.VMEM((NZ, NH - 1, part, wide), BF16),
            pltpu.VMEM((NZ, part, wide), BF16),
            pltpu.VMEM((rows, wide), BF16),
            dma((5,)),
            dma((2, NZ // 2)), dma((2, NZ // 2)),
            dma((2,)), dma((2,)),
            dma((2, NZ)), dma((2, NZ)),
            dma((2, NZ)), dma((2, NZ)),
            dma((2, 2, NZ)), dma((2, 2, NZ)),
            dma((2, NZ)), dma((2, NZ)),
            dma((3,)), dma((3,)),
            dma((2, NZ // 2, 2)), dma((2, NZ // 2, 2)),
            dma((NZ, 2, NX)), dma((NZ, NH - 1)),
            dma((NZ,)), dma((NH,)),
        ],
        compiler_params=pltpu.CompilerParams(
            collective_id=0, has_side_effects=True, vmem_limit_bytes=56 * 1024 * 1024
        ),
    )(
        block_order, kv_gain.reshape(LATENT // 128, 128), latent_keys.T,
        q_nope, q_rope, up_key, up_value, out_proj.T,
    )


def solution(mesh):
    return jax.shard_map(
        per_device,
        mesh=mesh,
        in_specs=(
            P("ctx", "head"),
            P("ctx", "head"),
            P("ctx", None),
            P(),
            P(None, "head"),
            P(None, "head"),
            P("head", "ctx"),
            P(),
        ),
        out_specs=P("ctx", "head"),
        check_vma=False,
    )
```

```python
import math

import jax
import jax.numpy as jnp
from jax import lax
from jax.experimental import pallas as pl
from jax.experimental.pallas import tpu as pltpu
from jax.sharding import PartitionSpec as P

NOPE = 128
ROPE = 64
VDIM = 128
LATENT = 512
CARRIED = LATENT + ROPE
BLOCKS = 64
WIDTH = CARRIED + BLOCKS
NZ = 8
NQ = 4
NX = 4
NH = 8
HIDDEN = -1e30
SCALE = math.log2(math.e) / (NOPE + ROPE) ** 0.5
MESH = pl.DeviceIdType.MESH
F32 = jnp.float32
BF16 = jnp.bfloat16

HALF_WIDTH = CARRIED // 2
Y_PIECES = ((0, 192), (192, 96))
X_PIECES = ((0, 144), (144, 144))
UNITS = (
    ((0, 0), (0, 2)),
    ((2, 0), (6, 0)),
    ((1, 0), (7, 0)),
    ((3, 0), (5, 0)),
    ((2, 2), (6, 2)),
    ((1, 2), (7, 2)),
    ((3, 2), (5, 2)),
    ((4, 0), (4, 2)),
)


def dot(a, b, dims=((1,), (0,))):
    return lax.dot_general(a, b, (dims, ((), ())), preferred_element_type=F32)


def slots_of(step):
    if step == 0:
        return (0,)
    if step == NZ // 2:
        return (step,)
    return (step, NZ - step)


def pick(table, i):
    value = jnp.int32(table[0])
    for n in range(1, len(table)):
        value = jnp.where(i == n, table[n], value)
    return value


def kernel(
    order_hbm, gain_hbm, latent_hbm, qn_hbm, qr_hbm, upk_hbm, upv_hbm, w_hbm, out,
    order, gain, latent, qn, qr, upk, upv, wbuf, kbuf, qbuf, acc, top, total, tri, abuf, pbuf, rsbuf, red,
    load_sem, kz_send, kz_recv, kn_send, kn_recv, kc_send, kc_recv, ky_send, ky_recv, kx_send, kx_recv,
    kd_send, kd_recv, w_send, w_recv, az_send, az_recv, rs_send, rs_recv, t_send, t_recv, heard,
):
    rows = latent.shape[1]
    half = rows // 2
    heads = upk.shape[1] // NOPE
    cols, depth = w_hbm.shape
    part = rows // NH
    last = NZ // 2
    ctx = lax.axis_index("ctx")
    head = lax.axis_index("head")
    z, q = lax.div(ctx, NQ), lax.rem(ctx, NQ)
    y_lo, core = lax.div(q, 2), lax.rem(q, 2)
    y_hi, x = lax.div(head, NX), lax.rem(head, NX)
    x_odd = lax.rem(x, 2)
    q_core = q + 1 - 2 * core
    q_y = lax.rem(q + 2, NQ)
    q_diag = q_y + 1 - 2 * core
    quads = (q, q_core, q_y, q_diag)

    def along_z(step):
        return lax.rem(z + step + NZ, NZ) * NQ + q, head

    def along_x(step):
        return ctx, y_hi * NX + lax.rem(x + step + NX, NX)

    to_core = (z * NQ + q_core, head)
    to_near = (z * NQ + q_y, head)
    to_far = (z * NQ + q_y, lax.rem(y_hi + 1, 2) * NX + x)

    def send(src, dst, send_sem, recv_sem, device):
        return pltpu.make_async_remote_copy(
            src_ref=src, dst_ref=dst, send_sem=send_sem, recv_sem=recv_sem,
            device_id=device, device_id_type=MESH,
        )

    loads = [
        pltpu.make_async_copy(src, dst, load_sem.at[n])
        for n, (src, dst) in enumerate(
            (
                (latent_hbm, latent), (gain_hbm, gain), (order_hbm, order), (qn_hbm, qn),
                (upk_hbm, upk), (qr_hbm, qr), (upv_hbm, upv), (w_hbm, wbuf.at[q]),
            )
        )
    ]
    loads[0].start()
    loads[1].start()

    nearest = [along_z(1), along_z(-1), along_z(2), along_z(-2), to_core, to_near, to_far]
    nearest += [along_x(1), along_x(-1)]
    barrier = pltpu.get_barrier_semaphore()
    for device in nearest:
        pl.semaphore_signal(barrier, inc=1, device_id=device, device_id_type=MESH)
    rounds = ((to_near, to_far), nearest[7:], nearest[7:], nearest[:4], nearest[2:4])

    def tell(n):
        for device in rounds[n]:
            pl.semaphore_signal(heard.at[n], inc=1, device_id=device, device_id_type=MESH)

    def hear(n):
        pl.semaphore_wait(heard.at[n], len(rounds[n]))
        if n + 1 < len(rounds):
            tell(n + 1)

    for load in loads[2:]:
        load.start()
    loads[0].wait()
    loads[1].wait()
    plain = latent[:LATENT].astype(F32)
    inverse = lax.rsqrt(jnp.mean(plain * plain, axis=0, keepdims=True) + 1e-06)
    for n in range(LATENT // 128):
        span = slice(n * 128, (n + 1) * 128)
        column = jnp.broadcast_to(gain[n : n + 1], (128, 128)).T
        kbuf[0, 0, span] = (plain[span] * inverse * column).astype(BF16)
    kbuf[0, 0, LATENT:CARRIED] = latent[LATENT:]

    def kept(odd, first, size):
        return pl.ds(pl.multiple_of(odd * HALF_WIDTH + first, 16), size)

    def kz(way, step):
        size = HALF_WIDTH if step < last else HALF_WIDTH // 2
        span = kept(x_odd, way * size if step == last else 0, size)
        hops, gone = (step, 0) if step < 3 else (step - 2, 2)
        source = (NZ - gone) % NZ if way == 0 else gone
        target = NZ - step if way == 0 else step
        return send(
            kbuf.at[source, 0, span], kbuf.at[target, 0, span],
            kz_send.at[way, step - 1], kz_recv.at[way, step - 1], along_z(hops * (1 - 2 * way)),
        )

    def kn(way):
        span = kept(1 - x_odd, 0, HALF_WIDTH)
        target = NZ - 1 if way == 0 else 1
        return send(
            kbuf.at[0, 0, span], kbuf.at[target, 0, span],
            kn_send.at[way], kn_recv.at[way], along_z(1 - 2 * way),
        )

    def kc(slot, n):
        span = kept(x_odd if n == 0 else 1 - x_odd, 0, HALF_WIDTH)
        return send(
            kbuf.at[slot, 0, span], kbuf.at[slot, 1, span],
            kc_send.at[n, slot], kc_recv.at[n, slot], to_core,
        )

    def ky(slot, n):
        span = kept(x_odd, *Y_PIECES[n])
        return send(
            kbuf.at[slot, 0, span], kbuf.at[slot, 2, span],
            ky_send.at[n, slot], ky_recv.at[n, slot], (to_far, to_near)[n],
        )

    def kx(quad, slot, n, coming=False):
        span = kept(1 - x_odd if coming else x_odd, *X_PIECES[n])
        return send(
            kbuf.at[slot, quad, span], kbuf.at[slot, quad, span],
            kx_send.at[quad // 2, n, slot], kx_recv.at[quad // 2, n, slot], along_x(1 - 2 * n),
        )

    def kd(slot, n):
        span = kept(x_odd if n == 0 else 1 - x_odd, 0, HALF_WIDTH)
        return send(
            kbuf.at[slot, 2, span], kbuf.at[slot, 3, span],
            kd_send.at[n, slot], kd_recv.at[n, slot], to_core,
        )

    w_core = send(w_hbm, wbuf.at[q], w_send.at[0], w_recv.at[0], to_core)
    w_near = send(w_hbm, wbuf.at[q], w_send.at[1], w_recv.at[1], to_near)
    w_diag = send(wbuf.at[q_y], wbuf.at[q_y], w_send.at[2], w_recv.at[2], to_core)

    def share(step):
        for slot in slots_of(step):
            for n in range(2):
                if step > 1:
                    kx(0, slot, n).start()
                ky(slot, n).start()
            kc(slot, 0).start()
            if step == 0:
                kc(slot, 1).start()

    def from_z(step):
        for way in range(2):
            kz(way, step).wait_recv()
        if step == 2:
            for way in range(2):
                kz(way, 3).start()
                kz(way, 4).start()
            for way in range(2):
                kn(way).start()
        share(step)

    def from_own_x(step):
        for slot in slots_of(step):
            if step == 1:
                kn(0 if slot > 1 else 1).wait_recv()
            else:
                for n in range(2):
                    kx(0, slot, n, True).wait_recv()
            kc(slot, 1).start()

    def from_y(step):
        for slot in slots_of(step):
            for n in range(2):
                ky(slot, n).wait_recv()
            for n in range(2):
                kx(2, slot, n).start()
            kd(slot, 0).start()

    def from_x(step):
        for slot in slots_of(step):
            for n in range(2):
                kx(2, slot, n, True).wait_recv()
            kd(slot, 1).start()

    def near_core(step):
        for slot in slots_of(step):
            kc(slot, 0).wait_recv()
            kc(slot, 1).wait_recv()

    def far_core(step):
        for slot in slots_of(step):
            kd(slot, 0).wait_recv()
            kd(slot, 1).wait_recv()

    pl.semaphore_wait(barrier, len(nearest))
    for step in (2, 1):
        for way in range(2):
            kz(way, step).start()
    share(0)
    w_near.start()
    w_core.start()
    tell(0)

    loads[2].wait()

    which = lax.broadcasted_iota(jnp.int32, (BLOCKS, rows), 0)
    first_half = lax.broadcasted_iota(jnp.int32, (BLOCKS, rows), 1) < half

    def mark(slot, carry):
        from_z = lax.rem(z + slot, NZ) * NQ
        for n, quad in enumerate(quads):
            there = 2 * (from_z + quad)
            owner = jnp.where(first_half, order[there], order[there + 1])
            kbuf[slot, n, CARRIED:] = jnp.where(which == owner, 1.0, 0.0).astype(BF16)
        return carry

    lax.fori_loop(0, NZ, mark, 0)
    lane = lax.broadcasted_iota(jnp.int32, (half, BLOCKS), 1)
    for r in range(2):
        row = lax.broadcasted_iota(jnp.int32, (half, rows), 0)
        key = lax.broadcasted_iota(jnp.int32, (half, rows), 1) - r * half
        tri[r] = jnp.where(jnp.logical_and(key > row, key < half), HIDDEN, 0.0)
    acc[...] = jnp.zeros_like(acc)
    total[...] = jnp.zeros_like(total)
    top[...] = jnp.full_like(top, HIDDEN)

    loads[3].wait()
    loads[4].wait()
    loads[5].wait()
    for n in range(heads):
        own = slice(n * NOPE, (n + 1) * NOPE)
        turned = dot(qn[:, own], upk[:, own], ((1,), (1,))).astype(BF16)
        rope = qr[:, n * ROPE : (n + 1) * ROPE]
        for r in range(2):
            span = slice((r * heads + n) * half, (r * heads + n + 1) * half)
            mine = slice(r * half, (r + 1) * half)
            later = jnp.where(lane > order[2 * ctx + r], HIDDEN, 0.0).astype(BF16)
            qbuf[span, :LATENT] = turned[mine]
            qbuf[span, LATENT:] = jnp.concatenate([rope[mine], later], axis=1)

    from_y(0)
    from_z(2)
    from_x(0)
    from_z(1)
    hear(0)

    def before_0():
        near_core(0)
        far_core(0)

    def before_1():
        from_own_x(2)
        from_z(3)
        from_y(2)
        near_core(2)
        hear(1)

    def before_2():
        from_z(4)
        from_own_x(1)
        from_y(1)
        from_own_x(3)
        near_core(1)
        hear(2)

    def before_3():
        from_y(3)
        from_x(2)
        from_y(4)
        near_core(3)
        hear(3)

    def before_4():
        from_own_x(4)
        from_x(1)
        far_core(2)

    def before_5():
        w_near.wait_recv()
        w_diag.start()
        from_x(3)
        from_x(4)
        far_core(1)
        hear(4)

    befores = (before_0, before_1, before_2, before_3, before_4, before_5)
    chunk = heads * half

    def soft(span, score, block):
        keys = score.shape[1]
        before = top[span]
        peak = jnp.maximum(before, jnp.max(score, axis=1, keepdims=True))
        fade = jnp.exp2((before - peak) * SCALE)
        expo = jnp.exp2((score - jnp.concatenate([peak] * (keys // 128), axis=1)) * SCALE)
        added = expo[:, :128]
        for n in range(1, keys // 128):
            added = added + expo[:, n * 128 : (n + 1) * 128]
        total[span] = total[span] * fade + added
        top[span] = peak
        faded = acc[span] * jnp.concatenate([fade] * (LATENT // 128), axis=1)
        acc[span] = faded + dot(expo.astype(BF16), block[:LATENT], ((1,), (1,)))

    def attend(i, carry):
        for n, before in enumerate(befores):
            pl.when(i == n)(before)
        pairs = [[pick([u[m][n] for u in UNITS], i) for n in range(2)] for m in range(2)]
        block = jnp.concatenate([kbuf[s, quad + n] for s, quad in pairs for n in range(2)], axis=1)
        spans = [slice(r * chunk, (r + 1) * chunk) for r in range(2)]
        scores = [dot(qbuf[span], block) for span in spans]
        for r in range(2):
            score = scores[r]
            own = (score[:, :rows].reshape(heads, half, rows) + tri[r][None]).reshape(chunk, rows)
            soft(spans[r], jnp.concatenate([own, score[:, rows:]], axis=1), block)

        @pl.when(i == 0)
        def _():
            tri[...] = jnp.zeros_like(tri)

        return carry

    lax.fori_loop(0, len(befores), attend, 0)
    loads[6].wait()
    loads[7].wait()
    near_core(4)
    far_core(3)
    far_core(4)

    def az(way, step, r):
        source = (NZ - step) % NZ if way == 0 else step
        target = (NZ - step - 1) % NZ if way == 0 else step + 1
        src, dst = abuf.at[source, r], abuf.at[target, r]
        if step == last - 1:
            span = pl.ds(way * (half // 2), half // 2)
            src, dst = src.at[span], dst.at[span]
        return send(
            src, dst, az_send.at[way, step, r], az_recv.at[way, step, r], along_z(1 - 2 * way),
        )

    for r in range(2):
        span = slice(r * chunk, (r + 1) * chunk)
        block = jnp.concatenate(
            [kbuf[s, quad + n] for u in UNITS[len(befores) :] for s, quad in u for n in range(2)],
            axis=1,
        )
        soft(span, dot(qbuf[span], block), block)
        for n in range(heads):
            mine = slice((r * heads + n) * half, (r * heads + n + 1) * half)
            own = slice(n * VDIM, (n + 1) * VDIM)
            wide = acc[mine]
            high = wide.astype(BF16)
            low = (wide - high.astype(F32)).astype(BF16)
            summed = dot(high, upv[:, own]) + dot(low, upv[:, own])
            weight = jnp.sum(total[mine], axis=1, keepdims=True)
            abuf[0, r, :, own] = (summed / weight).astype(BF16)
        az(0, 0, r).start()
        az(1, 0, r).start()

    w_core.wait_recv()
    w_diag.wait_recv()

    my_r = lax.rem(y_hi + x, 2)
    mine = pl.ds(pl.multiple_of(my_r * half + x * part, part), part)

    def scatter(slot, r, n):
        k = lax.rem(x + n, NX)
        owner_y = lax.rem(k + r, 2)
        other = lax.rem(owner_y + y_hi, 2)
        there = pl.ds(pl.multiple_of(r * half + k * part, part), part)
        place = n - 1 + NX * other if n > 0 else NX - 1
        return send(
            pbuf.at[slot, there], rsbuf.at[slot, place],
            rs_send.at[slot, r, n], rs_recv.at[slot, place], (ctx, owner_y * NX + k),
        )

    def project(slots, r):
        made = jnp.concatenate([abuf[slot, r] for slot in slots], axis=0)
        made = dot(made, wbuf[...].reshape(NQ * cols, depth), ((1,), (1,))).astype(BF16)
        for n, slot in enumerate(slots):
            pbuf[slot, r * half : (r + 1) * half] = made[n * half : (n + 1) * half]
        for slot in slots:
            pl.when(my_r != r)(scatter(slot, r, 0).start)
            for n in range(1, NX):
                scatter(slot, r, n).start()

    def home(slot):
        return send(
            red.at[slot], out.at[mine], t_send.at[slot], t_recv.at[head],
            (lax.rem(z + slot, NZ) * NQ + q, z),
        )

    def reduce(slot):
        value = pbuf[slot, mine].astype(F32)
        for n in range(NH - 1):
            send(
                red.at[slot], rsbuf.at[slot, n],
                rs_send.at[slot, 0, 0], rs_recv.at[slot, n], to_core,
            ).wait_recv()
            value = value + rsbuf[slot, n].astype(F32)
        red[slot] = value.astype(BF16)

    keep = pltpu.make_async_copy(red.at[0], out.at[mine], load_sem.at[len(loads)])

    def go_home(slot):
        if slot > 0:
            home(slot).start()
        else:
            pl.when(z != head)(home(0).start)

            pl.when(z == head)(keep.start)

    def sent_early():
        for way in range(2):
            for step in range(1, last + 1):
                kz(way, step).wait_send()
            kn(way).wait_send()
        for slot in range(NZ):
            for n in range(2):
                kc(slot, n).wait_send()
                ky(slot, n).wait_send()
                kx(2, slot, n).wait_send()
                if slot not in slots_of(0) + slots_of(1):
                    kx(0, slot, n).wait_send()
                kd(slot, n).wait_send()
        w_core.wait_send()
        w_near.wait_send()
        w_diag.wait_send()

    def sent(slots):
        for slot in slots:
            for r in range(2):
                pl.when(my_r != r)(scatter(slot, r, 0).wait_send)
                for n in range(1, NX):
                    scatter(slot, r, n).wait_send()
            if slot > 0:
                home(slot).wait_send()
            else:
                pl.when(z != head)(home(0).wait_send)
                pl.when(z == head)(keep.wait)

    for r in range(2):
        project((0,), r)
    sent_early()
    for step in range(1, last):
        for r in range(2):
            for way in range(2):
                az(way, step - 1, r).wait_recv()
            for way in range(2):
                az(way, step, r).start()
            project(slots_of(step), r)
        for slot in slots_of(step - 1):
            reduce(slot)
            go_home(slot)
        for way in range(2):
            for r in range(2):
                az(way, step - 1, r).wait_send()
    for r in range(2):
        for way in range(2):
            az(way, last - 1, r).wait_recv()
        project((last,), r)
    sent(slots_of(0) + slots_of(1))
    for slot in slots_of(last - 1) + slots_of(last):
        reduce(slot)
        go_home(slot)
    for way in range(2):
        for r in range(2):
            az(way, last - 1, r).wait_send()
    for step in range(2, last + 1):
        sent(slots_of(step))

    for n in range(NH):
        there = pl.ds((n // NX + n) % 2 * half + n % NX * part, part)
        arrival = send(red.at[0], out.at[there], t_send.at[0], t_recv.at[n], to_core)
        pl.when(jnp.logical_or(z != head, head != n))(arrival.wait_recv)


def per_device(q_nope, q_rope, latent_keys, kv_gain, up_key, up_value, out_proj, block_order):
    rows = q_nope.shape[0]
    heads = up_key.shape[1] // NOPE
    depth, cols = out_proj.shape
    wide = NQ * cols
    part = rows // NH
    dma = pltpu.SemaphoreType.DMA
    hbm = pl.BlockSpec(memory_space=pl.ANY)
    return pl.pallas_call(
        kernel,
        out_shape=jax.ShapeDtypeStruct((rows, wide), BF16),
        in_specs=[hbm] * 8,
        out_specs=hbm,
        scratch_shapes=[
            pltpu.SMEM(block_order.shape, jnp.int32),
            pltpu.VMEM((LATENT // 128, 128), F32),
            pltpu.VMEM(latent_keys.shape[::-1], BF16),
            pltpu.VMEM(q_nope.shape, BF16),
            pltpu.VMEM(q_rope.shape, BF16),
            pltpu.VMEM(up_key.shape, BF16),
            pltpu.VMEM(up_value.shape, BF16),
            pltpu.VMEM((NQ, cols, depth), BF16),
            pltpu.VMEM((NZ, NQ, WIDTH, rows), BF16),
            pltpu.VMEM((heads * rows, WIDTH), BF16),
            pltpu.VMEM((heads * rows, LATENT), F32),
            pltpu.VMEM((heads * rows, 128), F32),
            pltpu.VMEM((heads * rows, 128), F32),
            pltpu.VMEM((2, rows // 2, rows), F32),
            pltpu.VMEM((NZ, 2, rows // 2, heads * VDIM), BF16),
            pltpu.VMEM((NZ, rows, wide), BF16),
            pltpu.VMEM((NZ, NH - 1, part, wide), BF16),
            pltpu.VMEM((NZ, part, wide), BF16),
            dma((9,)),
            dma((2, NZ // 2)), dma((2, NZ // 2)),
            dma((2,)), dma((2,)),
            dma((2, NZ)), dma((2, NZ)),
            dma((2, NZ)), dma((2, NZ)),
            dma((2, 2, NZ)), dma((2, 2, NZ)),
            dma((2, NZ)), dma((2, NZ)),
            dma((3,)), dma((3,)),
            dma((2, NZ // 2, 2)), dma((2, NZ // 2, 2)),
            dma((NZ, 2, NX)), dma((NZ, NH - 1)),
            dma((NZ,)), dma((NH,)),
            pltpu.SemaphoreType.REGULAR((5,)),
        ],
        compiler_params=pltpu.CompilerParams(
            collective_id=0, has_side_effects=True, vmem_limit_bytes=56 * 1024 * 1024
        ),
    )(
        block_order, kv_gain.reshape(LATENT // 128, 128), latent_keys.T,
        q_nope, q_rope, up_key, up_value, out_proj.T,
    )


def solution(mesh):
    return jax.shard_map(
        per_device,
        mesh=mesh,
        in_specs=(
            P("ctx", "head"),
            P("ctx", "head"),
            P("ctx", None),
            P(),
            P(None, "head"),
            P(None, "head"),
            P("head", "ctx"),
            P(),
        ),
        out_specs=P("ctx", "head"),
        check_vma=False,
    )
```

```python
import math

import jax
import jax.numpy as jnp
from jax import lax
from jax.experimental import pallas as pl
from jax.experimental.pallas import tpu as pltpu
from jax.sharding import PartitionSpec as P

NOPE = 128
ROPE = 64
VDIM = 128
LATENT = 512
CARRIED = LATENT + ROPE
BLOCKS = 64
WIDTH = CARRIED + BLOCKS
NZ = 8
NQ = 4
NX = 4
NH = 8
HIDDEN = -1e30
SCALE = math.log2(math.e) / (NOPE + ROPE) ** 0.5
MESH = pl.DeviceIdType.MESH
F32 = jnp.float32
BF16 = jnp.bfloat16

HALF_WIDTH = CARRIED // 2
Y_PIECES = ((0, 288),)
X_PIECES = ((0, 144), (144, 144))
UNITS = (
    ((0, 0), (0, 2)),
    ((2, 0), (6, 0)),
    ((1, 0), (7, 0)),
    ((3, 0), (5, 0)),
    ((2, 2), (6, 2)),
    ((1, 2), (7, 2)),
    ((3, 2), (5, 2)),
    ((4, 0), (4, 2)),
)


def dot(a, b, dims=((1,), (0,))):
    return lax.dot_general(a, b, (dims, ((), ())), preferred_element_type=F32)


def slots_of(step):
    if step == 0:
        return (0,)
    if step == NZ // 2:
        return (step,)
    return (step, NZ - step)


def pick(table, i):
    value = jnp.int32(table[0])
    for n in range(1, len(table)):
        value = jnp.where(i == n, table[n], value)
    return value


def kernel(
    order_hbm, gain_hbm, latent_hbm, qn_hbm, qr_hbm, upk_hbm, upv_hbm, w_hbm, out,
    order, gain, latent, qn, qr, upk, upv, wbuf, kbuf, qbuf, acc, top, total, tri, abuf, pbuf, rsbuf, red,
    load_sem, kz_send, kz_recv, kn_send, kn_recv, kc_send, kc_recv, ky_send, ky_recv, kx_send, kx_recv,
    kd_send, kd_recv, w_send, w_recv, az_send, az_recv, rs_send, rs_recv, t_send, t_recv, heard,
):
    rows = latent.shape[1]
    half = rows // 2
    heads = upk.shape[1] // NOPE
    cols, depth = w_hbm.shape
    part = rows // NH
    last = NZ // 2
    ctx = lax.axis_index("ctx")
    head = lax.axis_index("head")
    z, q = lax.div(ctx, NQ), lax.rem(ctx, NQ)
    y_lo, core = lax.div(q, 2), lax.rem(q, 2)
    y_hi, x = lax.div(head, NX), lax.rem(head, NX)
    x_odd = lax.rem(x, 2)
    q_core = q + 1 - 2 * core
    q_y = lax.rem(q + 2, NQ)
    q_diag = q_y + 1 - 2 * core
    quads = (q, q_core, q_y, q_diag)

    def along_z(step):
        return lax.rem(z + step + NZ, NZ) * NQ + q, head

    def along_x(step):
        return ctx, y_hi * NX + lax.rem(x + step + NX, NX)

    to_core = (z * NQ + q_core, head)
    to_near = (z * NQ + q_y, head)
    to_far = (z * NQ + q_y, lax.rem(y_hi + 1, 2) * NX + x)

    def send(src, dst, send_sem, recv_sem, device):
        return pltpu.make_async_remote_copy(
            src_ref=src, dst_ref=dst, send_sem=send_sem, recv_sem=recv_sem,
            device_id=device, device_id_type=MESH,
        )

    loads = [
        pltpu.make_async_copy(src, dst, load_sem.at[n])
        for n, (src, dst) in enumerate(
            (
                (latent_hbm, latent), (gain_hbm, gain), (order_hbm, order), (qn_hbm, qn),
                (upk_hbm, upk), (qr_hbm, qr), (upv_hbm, upv), (w_hbm, wbuf.at[q]),
            )
        )
    ]
    loads[0].start()
    loads[1].start()

    nearest = [along_z(1), along_z(-1), along_z(2), along_z(-2), to_core, to_near, to_far]
    nearest += [along_x(1), along_x(-1)]
    barrier = pltpu.get_barrier_semaphore()
    for device in nearest:
        pl.semaphore_signal(barrier, inc=1, device_id=device, device_id_type=MESH)
    rounds = ((to_near, to_far), nearest[7:], nearest[7:], nearest[:4], nearest[2:4])

    def tell(n):
        for device in rounds[n]:
            pl.semaphore_signal(heard.at[n], inc=1, device_id=device, device_id_type=MESH)

    def hear(n):
        pl.semaphore_wait(heard.at[n], len(rounds[n]))
        if n + 1 < len(rounds):
            tell(n + 1)

    for load in loads[2:]:
        load.start()
    loads[0].wait()
    loads[1].wait()
    plain = latent[:LATENT].astype(F32)
    inverse = lax.rsqrt(jnp.mean(plain * plain, axis=0, keepdims=True) + 1e-06)
    for n in range(LATENT // 128):
        span = slice(n * 128, (n + 1) * 128)
        column = jnp.broadcast_to(gain[n : n + 1], (128, 128)).T
        kbuf[0, 0, span] = (plain[span] * inverse * column).astype(BF16)
    kbuf[0, 0, LATENT:CARRIED] = latent[LATENT:]

    def kept(odd, first, size):
        return pl.ds(pl.multiple_of(odd * HALF_WIDTH + first, 16), size)

    def kz(way, step):
        size = HALF_WIDTH if step < last else HALF_WIDTH // 2
        span = kept(x_odd, way * size if step == last else 0, size)
        hops, gone = (step, 0) if step < 3 else (step - 2, 2)
        source = (NZ - gone) % NZ if way == 0 else gone
        target = NZ - step if way == 0 else step
        return send(
            kbuf.at[source, 0, span], kbuf.at[target, 0, span],
            kz_send.at[way, step - 1], kz_recv.at[way, step - 1], along_z(hops * (1 - 2 * way)),
        )

    def kn(way):
        span = kept(1 - x_odd, 0, HALF_WIDTH)
        target = NZ - 1 if way == 0 else 1
        return send(
            kbuf.at[0, 0, span], kbuf.at[target, 0, span],
            kn_send.at[way], kn_recv.at[way], along_z(1 - 2 * way),
        )

    def kc(slot, n):
        span = kept(x_odd if n == 0 else 1 - x_odd, 0, HALF_WIDTH)
        return send(
            kbuf.at[slot, 0, span], kbuf.at[slot, 1, span],
            kc_send.at[n, slot], kc_recv.at[n, slot], to_core,
        )

    def ky(slot, n):
        span = kept(x_odd, *Y_PIECES[n])
        return send(
            kbuf.at[slot, 0, span], kbuf.at[slot, 2, span],
            ky_send.at[n, slot], ky_recv.at[n, slot], (to_far, to_near)[n],
        )

    def kx(quad, slot, n, coming=False):
        span = kept(1 - x_odd if coming else x_odd, *X_PIECES[n])
        return send(
            kbuf.at[slot, quad, span], kbuf.at[slot, quad, span],
            kx_send.at[quad // 2, n, slot], kx_recv.at[quad // 2, n, slot], along_x(1 - 2 * n),
        )

    def kd(slot, n):
        span = kept(x_odd if n == 0 else 1 - x_odd, 0, HALF_WIDTH)
        return send(
            kbuf.at[slot, 2, span], kbuf.at[slot, 3, span],
            kd_send.at[n, slot], kd_recv.at[n, slot], to_core,
        )

    w_core = send(w_hbm, wbuf.at[q], w_send.at[0], w_recv.at[0], to_core)
    w_near = send(w_hbm, wbuf.at[q], w_send.at[1], w_recv.at[1], to_near)
    w_diag = send(wbuf.at[q_y], wbuf.at[q_y], w_send.at[2], w_recv.at[2], to_core)

    def share(step):
        for slot in slots_of(step):
            for n in range(2):
                if step > 1:
                    kx(0, slot, n).start()
                if n < len(Y_PIECES):
                    ky(slot, n).start()
            kc(slot, 0).start()
            if step == 0:
                kc(slot, 1).start()

    def from_z(step):
        for way in range(2):
            kz(way, step).wait_recv()
        if step == 2:
            for way in range(2):
                kz(way, 3).start()
                kz(way, 4).start()
            for way in range(2):
                kn(way).start()
        share(step)

    def from_own_x(step):
        for slot in slots_of(step):
            if step == 1:
                kn(0 if slot > 1 else 1).wait_recv()
            else:
                for n in range(2):
                    kx(0, slot, n, True).wait_recv()
            kc(slot, 1).start()

    def from_y(step):
        for slot in slots_of(step):
            for n in range(len(Y_PIECES)):
                ky(slot, n).wait_recv()
            for n in range(2):
                kx(2, slot, n).start()
            kd(slot, 0).start()

    def from_x(step):
        for slot in slots_of(step):
            for n in range(2):
                kx(2, slot, n, True).wait_recv()
            kd(slot, 1).start()

    def near_core(step):
        for slot in slots_of(step):
            kc(slot, 0).wait_recv()
            kc(slot, 1).wait_recv()

    def far_core(step):
        for slot in slots_of(step):
            kd(slot, 0).wait_recv()
            kd(slot, 1).wait_recv()

    pl.semaphore_wait(barrier, len(nearest))
    for step in (2, 1):
        for way in range(2):
            kz(way, step).start()
    share(0)
    w_near.start()
    w_core.start()
    tell(0)

    loads[2].wait()

    which = lax.broadcasted_iota(jnp.int32, (BLOCKS, rows), 0)
    first_half = lax.broadcasted_iota(jnp.int32, (BLOCKS, rows), 1) < half

    def mark(slot, carry):
        from_z = lax.rem(z + slot, NZ) * NQ
        for n, quad in enumerate(quads):
            there = 2 * (from_z + quad)
            owner = jnp.where(first_half, order[there], order[there + 1])
            kbuf[slot, n, CARRIED:] = jnp.where(which == owner, 1.0, 0.0).astype(BF16)
        return carry

    lax.fori_loop(0, NZ, mark, 0)
    lane = lax.broadcasted_iota(jnp.int32, (half, BLOCKS), 1)
    for r in range(2):
        row = lax.broadcasted_iota(jnp.int32, (half, rows), 0)
        key = lax.broadcasted_iota(jnp.int32, (half, rows), 1) - r * half
        tri[r] = jnp.where(jnp.logical_and(key > row, key < half), HIDDEN, 0.0)
    acc[...] = jnp.zeros_like(acc)
    total[...] = jnp.zeros_like(total)
    top[...] = jnp.full_like(top, HIDDEN)

    loads[3].wait()
    loads[4].wait()
    loads[5].wait()
    for n in range(heads):
        own = slice(n * NOPE, (n + 1) * NOPE)
        turned = dot(qn[:, own], upk[:, own], ((1,), (1,))).astype(BF16)
        rope = qr[:, n * ROPE : (n + 1) * ROPE]
        for r in range(2):
            span = slice((r * heads + n) * half, (r * heads + n + 1) * half)
            mine = slice(r * half, (r + 1) * half)
            later = jnp.where(lane > order[2 * ctx + r], HIDDEN, 0.0).astype(BF16)
            qbuf[span, :LATENT] = turned[mine]
            qbuf[span, LATENT:] = jnp.concatenate([rope[mine], later], axis=1)

    from_y(0)
    from_z(2)
    from_x(0)
    from_z(1)
    hear(0)

    def before_0():
        near_core(0)
        far_core(0)

    def before_1():
        from_own_x(2)
        from_z(3)
        from_y(2)
        near_core(2)
        hear(1)

    def before_2():
        from_z(4)
        from_own_x(1)
        from_y(1)
        from_own_x(3)
        near_core(1)
        hear(2)

    def before_3():
        from_y(3)
        from_x(2)
        from_y(4)
        near_core(3)
        hear(3)

    def before_4():
        from_own_x(4)
        from_x(1)
        far_core(2)

    def before_5():
        w_near.wait_recv()
        w_diag.start()
        from_x(3)
        from_x(4)
        far_core(1)
        hear(4)

    befores = (before_0, before_1, before_2, before_3, before_4, before_5)
    chunk = heads * half

    def soft(span, score, block):
        keys = score.shape[1]
        before = top[span]
        peak = jnp.maximum(before, jnp.max(score, axis=1, keepdims=True))
        fade = jnp.exp2((before - peak) * SCALE)
        expo = jnp.exp2((score - jnp.concatenate([peak] * (keys // 128), axis=1)) * SCALE)
        added = expo[:, :128]
        for n in range(1, keys // 128):
            added = added + expo[:, n * 128 : (n + 1) * 128]
        total[span] = total[span] * fade + added
        top[span] = peak
        faded = acc[span] * jnp.concatenate([fade] * (LATENT // 128), axis=1)
        acc[span] = faded + dot(expo.astype(BF16), block[:LATENT], ((1,), (1,)))

    def attend(i, carry):
        for n, before in enumerate(befores):
            pl.when(i == n)(before)
        pairs = [[pick([u[m][n] for u in UNITS], i) for n in range(2)] for m in range(2)]
        block = jnp.concatenate([kbuf[s, quad + n] for s, quad in pairs for n in range(2)], axis=1)
        spans = [slice(r * chunk, (r + 1) * chunk) for r in range(2)]
        scores = [dot(qbuf[span], block) for span in spans]
        for r in range(2):
            score = scores[r]
            own = (score[:, :rows].reshape(heads, half, rows) + tri[r][None]).reshape(chunk, rows)
            soft(spans[r], jnp.concatenate([own, score[:, rows:]], axis=1), block)

        @pl.when(i == 0)
        def _():
            tri[...] = jnp.zeros_like(tri)

        return carry

    lax.fori_loop(0, len(befores), attend, 0)
    loads[6].wait()
    loads[7].wait()
    near_core(4)
    far_core(3)
    far_core(4)

    def az(way, step, r):
        source = (NZ - step) % NZ if way == 0 else step
        target = (NZ - step - 1) % NZ if way == 0 else step + 1
        src, dst = abuf.at[source, r], abuf.at[target, r]
        if step == last - 1:
            span = pl.ds(way * (half // 2), half // 2)
            src, dst = src.at[span], dst.at[span]
        return send(
            src, dst, az_send.at[way, step, r], az_recv.at[way, step, r], along_z(1 - 2 * way),
        )

    for r in range(2):
        span = slice(r * chunk, (r + 1) * chunk)
        block = jnp.concatenate(
            [kbuf[s, quad + n] for u in UNITS[len(befores) :] for s, quad in u for n in range(2)],
            axis=1,
        )
        soft(span, dot(qbuf[span], block), block)
        for n in range(heads):
            mine = slice((r * heads + n) * half, (r * heads + n + 1) * half)
            own = slice(n * VDIM, (n + 1) * VDIM)
            wide = acc[mine]
            high = wide.astype(BF16)
            low = (wide - high.astype(F32)).astype(BF16)
            summed = dot(high, upv[:, own]) + dot(low, upv[:, own])
            weight = jnp.sum(total[mine], axis=1, keepdims=True)
            abuf[0, r, :, own] = (summed / weight).astype(BF16)
        az(0, 0, r).start()
        az(1, 0, r).start()

    w_core.wait_recv()
    w_diag.wait_recv()

    my_r = lax.rem(y_hi + x, 2)
    mine = pl.ds(pl.multiple_of(my_r * half + x * part, part), part)

    def scatter(slot, r, n):
        k = lax.rem(x + n, NX)
        owner_y = lax.rem(k + r, 2)
        other = lax.rem(owner_y + y_hi, 2)
        there = pl.ds(pl.multiple_of(r * half + k * part, part), part)
        place = n - 1 + NX * other if n > 0 else NX - 1
        return send(
            pbuf.at[slot, there], rsbuf.at[slot, place],
            rs_send.at[slot, r, n], rs_recv.at[slot, place], (ctx, owner_y * NX + k),
        )

    def project(slots, r):
        made = jnp.concatenate([abuf[slot, r] for slot in slots], axis=0)
        made = dot(made, wbuf[...].reshape(NQ * cols, depth), ((1,), (1,))).astype(BF16)
        for n, slot in enumerate(slots):
            pbuf[slot, r * half : (r + 1) * half] = made[n * half : (n + 1) * half]
        for slot in slots:
            pl.when(my_r != r)(scatter(slot, r, 0).start)
            for n in range(1, NX):
                scatter(slot, r, n).start()

    def home(slot):
        return send(
            red.at[slot], out.at[mine], t_send.at[slot], t_recv.at[head],
            (lax.rem(z + slot, NZ) * NQ + q, z),
        )

    def reduce(slot):
        value = pbuf[slot, mine].astype(F32)
        for n in range(NH - 1):
            send(
                red.at[slot], rsbuf.at[slot, n],
                rs_send.at[slot, 0, 0], rs_recv.at[slot, n], to_core,
            ).wait_recv()
            value = value + rsbuf[slot, n].astype(F32)
        red[slot] = value.astype(BF16)

    keep = pltpu.make_async_copy(red.at[0], out.at[mine], load_sem.at[len(loads)])

    def go_home(slot):
        if slot > 0:
            home(slot).start()
        else:
            pl.when(z != head)(home(0).start)

            pl.when(z == head)(keep.start)

    def sent_early():
        for way in range(2):
            for step in range(1, last + 1):
                kz(way, step).wait_send()
            kn(way).wait_send()
        for slot in range(NZ):
            for n in range(2):
                kc(slot, n).wait_send()
                if n < len(Y_PIECES):
                    ky(slot, n).wait_send()
                kx(2, slot, n).wait_send()
                if slot not in slots_of(0) + slots_of(1):
                    kx(0, slot, n).wait_send()
                kd(slot, n).wait_send()
        w_core.wait_send()
        w_near.wait_send()
        w_diag.wait_send()

    def sent(slots):
        for slot in slots:
            for r in range(2):
                pl.when(my_r != r)(scatter(slot, r, 0).wait_send)
                for n in range(1, NX):
                    scatter(slot, r, n).wait_send()
            if slot > 0:
                home(slot).wait_send()
            else:
                pl.when(z != head)(home(0).wait_send)
                pl.when(z == head)(keep.wait)

    def finish(slots):
        for slot in slots:
            reduce(slot)
            go_home(slot)

    for r in range(2):
        project((0,), r)
    sent_early()
    for step in range(1, last):
        for r in range(2):
            for way in range(2):
                az(way, step - 1, r).wait_recv()
            for way in range(2):
                az(way, step, r).start()
            project(slots_of(step), r)
            if r == 0 and step > 1:
                finish(slots_of(step - 2))
        for way in range(2):
            for r in range(2):
                az(way, step - 1, r).wait_send()
    for r in range(2):
        for way in range(2):
            az(way, last - 1, r).wait_recv()
        project((last,), r)
        if r == 0:
            finish(slots_of(last - 2))
    finish(slots_of(last - 1) + slots_of(last))
    for n in range(NH):
        there = pl.ds((n // NX + n) % 2 * half + n % NX * part, part)
        arrival = send(red.at[0], out.at[there], t_send.at[0], t_recv.at[n], to_core)
        pl.when(jnp.logical_or(z != head, head != n))(arrival.wait_recv)
    for way in range(2):
        for r in range(2):
            az(way, last - 1, r).wait_send()
    for step in range(last + 1):
        sent(slots_of(step))


def per_device(q_nope, q_rope, latent_keys, kv_gain, up_key, up_value, out_proj, block_order):
    rows = q_nope.shape[0]
    heads = up_key.shape[1] // NOPE
    depth, cols = out_proj.shape
    wide = NQ * cols
    part = rows // NH
    dma = pltpu.SemaphoreType.DMA
    hbm = pl.BlockSpec(memory_space=pl.ANY)
    return pl.pallas_call(
        kernel,
        out_shape=jax.ShapeDtypeStruct((rows, wide), BF16),
        in_specs=[hbm] * 8,
        out_specs=hbm,
        scratch_shapes=[
            pltpu.SMEM(block_order.shape, jnp.int32),
            pltpu.VMEM((LATENT // 128, 128), F32),
            pltpu.VMEM(latent_keys.shape[::-1], BF16),
            pltpu.VMEM(q_nope.shape, BF16),
            pltpu.VMEM(q_rope.shape, BF16),
            pltpu.VMEM(up_key.shape, BF16),
            pltpu.VMEM(up_value.shape, BF16),
            pltpu.VMEM((NQ, cols, depth), BF16),
            pltpu.VMEM((NZ, NQ, WIDTH, rows), BF16),
            pltpu.VMEM((heads * rows, WIDTH), BF16),
            pltpu.VMEM((heads * rows, LATENT), F32),
            pltpu.VMEM((heads * rows, 128), F32),
            pltpu.VMEM((heads * rows, 128), F32),
            pltpu.VMEM((2, rows // 2, rows), F32),
            pltpu.VMEM((NZ, 2, rows // 2, heads * VDIM), BF16),
            pltpu.VMEM((NZ, rows, wide), BF16),
            pltpu.VMEM((NZ, NH - 1, part, wide), BF16),
            pltpu.VMEM((NZ, part, wide), BF16),
            dma((9,)),
            dma((2, NZ // 2)), dma((2, NZ // 2)),
            dma((2,)), dma((2,)),
            dma((2, NZ)), dma((2, NZ)),
            dma((2, NZ)), dma((2, NZ)),
            dma((2, 2, NZ)), dma((2, 2, NZ)),
            dma((2, NZ)), dma((2, NZ)),
            dma((3,)), dma((3,)),
            dma((2, NZ // 2, 2)), dma((2, NZ // 2, 2)),
            dma((NZ, 2, NX)), dma((NZ, NH - 1)),
            dma((NZ,)), dma((NH,)),
            pltpu.SemaphoreType.REGULAR((5,)),
        ],
        compiler_params=pltpu.CompilerParams(
            collective_id=0, has_side_effects=True, vmem_limit_bytes=56 * 1024 * 1024
        ),
    )(
        block_order, kv_gain.reshape(LATENT // 128, 128), latent_keys.T,
        q_nope, q_rope, up_key, up_value, out_proj.T,
    )


def solution(mesh):
    return jax.shard_map(
        per_device,
        mesh=mesh,
        in_specs=(
            P("ctx", "head"),
            P("ctx", "head"),
            P("ctx", None),
            P(),
            P(None, "head"),
            P(None, "head"),
            P("head", "ctx"),
            P(),
        ),
        out_specs=P("ctx", "head"),
        check_vma=False,
    )
```

```python
import math

import jax
import jax.numpy as jnp
from jax import lax
from jax.experimental import pallas as pl
from jax.experimental.pallas import tpu as pltpu
from jax.sharding import PartitionSpec as P

NOPE = 128
ROPE = 64
VDIM = 128
LATENT = 512
CARRIED = LATENT + ROPE
BLOCKS = 64
WIDTH = CARRIED + BLOCKS
NZ = 8
NQ = 4
NX = 4
NH = 8
HIDDEN = -1e30
SCALE = math.log2(math.e) / (NOPE + ROPE) ** 0.5
MESH = pl.DeviceIdType.MESH
F32 = jnp.float32
BF16 = jnp.bfloat16

HALF_WIDTH = CARRIED // 2
Y_PIECES = ((0, 288),)
X_PIECES = ((0, 144), (144, 144))
UNITS = (
    ((0, 0), (0, 2)),
    ((2, 0), (6, 0)),
    ((1, 0), (7, 0)),
    ((3, 0), (5, 0)),
    ((2, 2), (6, 2)),
    ((1, 2), (7, 2)),
    ((3, 2), (5, 2)),
    ((4, 0), (4, 2)),
)


def dot(a, b, dims=((1,), (0,))):
    return lax.dot_general(a, b, (dims, ((), ())), preferred_element_type=F32)


def slots_of(step):
    if step == 0:
        return (0,)
    if step == NZ // 2:
        return (step,)
    return (step, NZ - step)


def pick(table, i):
    value = jnp.int32(table[0])
    for n in range(1, len(table)):
        value = jnp.where(i == n, table[n], value)
    return value


def kernel(
    order_hbm, gain_hbm, latent_hbm, qn_hbm, qr_hbm, upk_hbm, upv_hbm, w_hbm, out,
    order, gain, latent, qn, qr, upk, upv, wbuf, kbuf, qbuf, acc, top, total, tri, abuf, pbuf, rsbuf, red,
    load_sem, kz_send, kz_recv, kn_send, kn_recv, kc_send, kc_recv, ky_send, ky_recv, kx_send, kx_recv,
    kd_send, kd_recv, w_send, w_recv, az_send, az_recv, rs_send, rs_recv, t_send, t_recv, heard,
):
    rows = latent.shape[1]
    half = rows // 2
    heads = upk.shape[1] // NOPE
    cols, depth = w_hbm.shape
    part = rows // NH
    last = NZ // 2
    ctx = lax.axis_index("ctx")
    head = lax.axis_index("head")
    z, q = lax.div(ctx, NQ), lax.rem(ctx, NQ)
    y_lo, core = lax.div(q, 2), lax.rem(q, 2)
    y_hi, x = lax.div(head, NX), lax.rem(head, NX)
    x_odd = lax.rem(x, 2)
    q_core = q + 1 - 2 * core
    q_y = lax.rem(q + 2, NQ)
    q_diag = q_y + 1 - 2 * core
    quads = (q, q_core, q_y, q_diag)

    def along_z(step):
        return lax.rem(z + step + NZ, NZ) * NQ + q, head

    def along_x(step):
        return ctx, y_hi * NX + lax.rem(x + step + NX, NX)

    to_core = (z * NQ + q_core, head)
    to_near = (z * NQ + q_y, head)
    to_far = (z * NQ + q_y, lax.rem(y_hi + 1, 2) * NX + x)

    def send(src, dst, send_sem, recv_sem, device):
        return pltpu.make_async_remote_copy(
            src_ref=src, dst_ref=dst, send_sem=send_sem, recv_sem=recv_sem,
            device_id=device, device_id_type=MESH,
        )

    loads = [
        pltpu.make_async_copy(src, dst, load_sem.at[n])
        for n, (src, dst) in enumerate(
            (
                (latent_hbm, latent), (gain_hbm, gain), (order_hbm, order), (qn_hbm, qn),
                (upk_hbm, upk), (qr_hbm, qr), (upv_hbm, upv), (w_hbm, wbuf.at[q]),
            )
        )
    ]
    loads[0].start()
    loads[1].start()

    nearest = [along_z(1), along_z(-1), along_z(2), along_z(-2), to_core, to_near, to_far]
    nearest += [along_x(1), along_x(-1)]
    barrier = pltpu.get_barrier_semaphore()
    for device in nearest:
        pl.semaphore_signal(barrier, inc=1, device_id=device, device_id_type=MESH)
    rounds = ((to_near, to_far), nearest[7:], nearest[7:], nearest[:4], nearest[2:4])

    def tell(n):
        for device in rounds[n]:
            pl.semaphore_signal(heard.at[n], inc=1, device_id=device, device_id_type=MESH)

    def hear(n):
        pl.semaphore_wait(heard.at[n], len(rounds[n]))
        if n + 1 < len(rounds):
            tell(n + 1)

    for load in loads[2:]:
        load.start()
    loads[0].wait()
    loads[1].wait()
    plain = latent[:LATENT].astype(F32)
    inverse = lax.rsqrt(jnp.mean(plain * plain, axis=0, keepdims=True) + 1e-06)
    for n in range(LATENT // 128):
        span = slice(n * 128, (n + 1) * 128)
        column = jnp.broadcast_to(gain[n : n + 1], (128, 128)).T
        kbuf[0, 0, span] = (plain[span] * inverse * column).astype(BF16)
    kbuf[0, 0, LATENT:CARRIED] = latent[LATENT:]

    def kept(odd, first, size):
        return pl.ds(pl.multiple_of(odd * HALF_WIDTH + first, 16), size)

    def kz(way, step):
        size = HALF_WIDTH if step < last else HALF_WIDTH // 2
        span = kept(x_odd, way * size if step == last else 0, size)
        hops, gone = (step, 0) if step < 3 else (step - 2, 2)
        source = (NZ - gone) % NZ if way == 0 else gone
        target = NZ - step if way == 0 else step
        return send(
            kbuf.at[source, 0, span], kbuf.at[target, 0, span],
            kz_send.at[way, step - 1], kz_recv.at[way, step - 1], along_z(hops * (1 - 2 * way)),
        )

    def kn(way):
        span = kept(1 - x_odd, 0, HALF_WIDTH)
        target = NZ - 1 if way == 0 else 1
        return send(
            kbuf.at[0, 0, span], kbuf.at[target, 0, span],
            kn_send.at[way], kn_recv.at[way], along_z(1 - 2 * way),
        )

    def kc(slot, n):
        span = kept(x_odd if n == 0 else 1 - x_odd, 0, HALF_WIDTH)
        return send(
            kbuf.at[slot, 0, span], kbuf.at[slot, 1, span],
            kc_send.at[n, slot], kc_recv.at[n, slot], to_core,
        )

    def ky(slot, n):
        span = kept(x_odd, *Y_PIECES[n])
        return send(
            kbuf.at[slot, 0, span], kbuf.at[slot, 2, span],
            ky_send.at[n, slot], ky_recv.at[n, slot], (to_far, to_near)[n],
        )

    def kx(quad, slot, n, coming=False):
        span = kept(1 - x_odd if coming else x_odd, *X_PIECES[n])
        return send(
            kbuf.at[slot, quad, span], kbuf.at[slot, quad, span],
            kx_send.at[quad // 2, n, slot], kx_recv.at[quad // 2, n, slot], along_x(1 - 2 * n),
        )

    def kd(slot, n):
        span = kept(x_odd if n == 0 else 1 - x_odd, 0, HALF_WIDTH)
        return send(
            kbuf.at[slot, 2, span], kbuf.at[slot, 3, span],
            kd_send.at[n, slot], kd_recv.at[n, slot], to_core,
        )

    w_core = send(w_hbm, wbuf.at[q], w_send.at[0], w_recv.at[0], to_core)
    w_near = send(w_hbm, wbuf.at[q], w_send.at[1], w_recv.at[1], to_near)
    w_diag = send(wbuf.at[q_y], wbuf.at[q_y], w_send.at[2], w_recv.at[2], to_core)

    def share(step):
        for slot in slots_of(step):
            for n in range(2):
                if step > 1:
                    kx(0, slot, n).start()
                if n < len(Y_PIECES):
                    ky(slot, n).start()
            kc(slot, 0).start()
            if step == 0:
                kc(slot, 1).start()

    def from_z(step):
        for way in range(2):
            kz(way, step).wait_recv()
        if step == 2:
            for way in range(2):
                kz(way, 3).start()
                kz(way, 4).start()
            for way in range(2):
                kn(way).start()
        share(step)

    def from_own_x(step):
        for slot in slots_of(step):
            if step == 1:
                kn(0 if slot > 1 else 1).wait_recv()
            else:
                for n in range(2):
                    kx(0, slot, n, True).wait_recv()
            kc(slot, 1).start()

    def from_y(step):
        for slot in slots_of(step):
            for n in range(len(Y_PIECES)):
                ky(slot, n).wait_recv()
            for n in range(2):
                kx(2, slot, n).start()
            kd(slot, 0).start()

    def from_x(step):
        for slot in slots_of(step):
            for n in range(2):
                kx(2, slot, n, True).wait_recv()
            kd(slot, 1).start()

    def near_core(step):
        for slot in slots_of(step):
            kc(slot, 0).wait_recv()
            kc(slot, 1).wait_recv()

    def far_core(step):
        for slot in slots_of(step):
            kd(slot, 0).wait_recv()
            kd(slot, 1).wait_recv()

    pl.semaphore_wait(barrier, len(nearest))
    for step in (2, 1):
        for way in range(2):
            kz(way, step).start()
    share(0)
    w_near.start()
    tell(0)

    loads[2].wait()

    which = lax.broadcasted_iota(jnp.int32, (BLOCKS, rows), 0)
    first_half = lax.broadcasted_iota(jnp.int32, (BLOCKS, rows), 1) < half

    def mark(slot, carry):
        from_z = lax.rem(z + slot, NZ) * NQ
        for n, quad in enumerate(quads):
            there = 2 * (from_z + quad)
            owner = jnp.where(first_half, order[there], order[there + 1])
            kbuf[slot, n, CARRIED:] = jnp.where(which == owner, 1.0, 0.0).astype(BF16)
        return carry

    lax.fori_loop(0, NZ, mark, 0)
    lane = lax.broadcasted_iota(jnp.int32, (half, BLOCKS), 1)
    for r in range(2):
        row = lax.broadcasted_iota(jnp.int32, (half, rows), 0)
        key = lax.broadcasted_iota(jnp.int32, (half, rows), 1) - r * half
        tri[r] = jnp.where(jnp.logical_and(key > row, key < half), HIDDEN, 0.0)
    acc[...] = jnp.zeros_like(acc)
    total[...] = jnp.zeros_like(total)
    top[...] = jnp.full_like(top, HIDDEN)

    loads[3].wait()
    loads[4].wait()
    loads[5].wait()
    for n in range(heads):
        own = slice(n * NOPE, (n + 1) * NOPE)
        turned = dot(qn[:, own], upk[:, own], ((1,), (1,))).astype(BF16)
        rope = qr[:, n * ROPE : (n + 1) * ROPE]
        for r in range(2):
            span = slice((r * heads + n) * half, (r * heads + n + 1) * half)
            mine = slice(r * half, (r + 1) * half)
            later = jnp.where(lane > order[2 * ctx + r], HIDDEN, 0.0).astype(BF16)
            qbuf[span, :LATENT] = turned[mine]
            qbuf[span, LATENT:] = jnp.concatenate([rope[mine], later], axis=1)

    from_y(0)
    from_z(2)
    from_x(0)
    from_z(1)
    hear(0)

    def before_0():
        near_core(0)
        far_core(0)

    def before_1():
        from_own_x(2)
        from_z(3)
        from_y(2)
        near_core(2)
        w_core.start()
        hear(1)

    def before_2():
        from_z(4)
        from_own_x(1)
        from_y(1)
        from_own_x(3)
        near_core(1)
        hear(2)

    def before_3():
        from_y(3)
        from_x(2)
        from_y(4)
        near_core(3)
        hear(3)

    def before_4():
        w_near.wait_recv()
        w_diag.start()
        from_own_x(4)
        from_x(1)
        far_core(2)

    def before_5():
        from_x(3)
        from_x(4)
        far_core(1)
        hear(4)

    befores = (before_0, before_1, before_2, before_3, before_4)
    chunk = heads * half

    def soft(span, score, block):
        keys = score.shape[1]
        before = top[span]
        peak = jnp.maximum(before, jnp.max(score, axis=1, keepdims=True))
        fade = jnp.exp2((before - peak) * SCALE)
        expo = jnp.exp2((score - jnp.concatenate([peak] * (keys // 128), axis=1)) * SCALE)
        added = expo[:, :128]
        for n in range(1, keys // 128):
            added = added + expo[:, n * 128 : (n + 1) * 128]
        total[span] = total[span] * fade + added
        top[span] = peak
        faded = acc[span] * jnp.concatenate([fade] * (LATENT // 128), axis=1)
        acc[span] = faded + dot(expo.astype(BF16), block[:LATENT], ((1,), (1,)))

    def attend(i, carry):
        for n, before in enumerate(befores):
            pl.when(i == n)(before)
        pairs = [[pick([u[m][n] for u in UNITS], i) for n in range(2)] for m in range(2)]
        block = jnp.concatenate([kbuf[s, quad + n] for s, quad in pairs for n in range(2)], axis=1)
        spans = [slice(r * chunk, (r + 1) * chunk) for r in range(2)]
        scores = [dot(qbuf[span], block) for span in spans]
        for r in range(2):
            score = scores[r]
            own = (score[:, :rows].reshape(heads, half, rows) + tri[r][None]).reshape(chunk, rows)
            soft(spans[r], jnp.concatenate([own, score[:, rows:]], axis=1), block)

        @pl.when(i == 0)
        def _():
            tri[...] = jnp.zeros_like(tri)

        return carry

    lax.fori_loop(0, len(befores), attend, 0)
    before_5()
    loads[6].wait()
    loads[7].wait()

    def blocks(units):
        return jnp.concatenate(
            [kbuf[s, quad + n] for u in units for s, quad in u for n in range(2)], axis=1
        )

    ahead = len(befores)
    block = blocks(UNITS[ahead : ahead + 1])
    soft(slice(0, chunk), dot(qbuf[:chunk], block), block)
    near_core(4)
    far_core(3)
    far_core(4)

    def az(way, step, r):
        source = (NZ - step) % NZ if way == 0 else step
        target = (NZ - step - 1) % NZ if way == 0 else step + 1
        src, dst = abuf.at[source, r], abuf.at[target, r]
        if step == last - 1:
            span = pl.ds(way * (half // 2), half // 2)
            src, dst = src.at[span], dst.at[span]
        return send(
            src, dst, az_send.at[way, step, r], az_recv.at[way, step, r], along_z(1 - 2 * way),
        )

    for r in range(2):
        span = slice(r * chunk, (r + 1) * chunk)
        block = blocks(UNITS[ahead + 1 - r :])
        soft(span, dot(qbuf[span], block), block)
        for n in range(heads):
            mine = slice((r * heads + n) * half, (r * heads + n + 1) * half)
            own = slice(n * VDIM, (n + 1) * VDIM)
            wide = acc[mine]
            high = wide.astype(BF16)
            low = (wide - high.astype(F32)).astype(BF16)
            summed = dot(high, upv[:, own]) + dot(low, upv[:, own])
            weight = jnp.sum(total[mine], axis=1, keepdims=True)
            abuf[0, r, :, own] = (summed / weight).astype(BF16)
        az(0, 0, r).start()
        az(1, 0, r).start()

    w_core.wait_recv()
    w_diag.wait_recv()

    my_r = lax.rem(y_hi + x, 2)
    mine = pl.ds(pl.multiple_of(my_r * half + x * part, part), part)

    def scatter(slot, r, n):
        k = lax.rem(x + n, NX)
        owner_y = lax.rem(k + r, 2)
        other = lax.rem(owner_y + y_hi, 2)
        there = pl.ds(pl.multiple_of(r * half + k * part, part), part)
        place = n - 1 + NX * other if n > 0 else NX - 1
        return send(
            pbuf.at[slot, there], rsbuf.at[slot, place],
            rs_send.at[slot, r, n], rs_recv.at[slot, place], (ctx, owner_y * NX + k),
        )

    def project(slots, r):
        made = jnp.concatenate([abuf[slot, r] for slot in slots], axis=0)
        made = dot(made, wbuf[...].reshape(NQ * cols, depth), ((1,), (1,))).astype(BF16)
        for n, slot in enumerate(slots):
            pbuf[slot, r * half : (r + 1) * half] = made[n * half : (n + 1) * half]
        for slot in slots:
            pl.when(my_r != r)(scatter(slot, r, 0).start)
            for n in range(1, NX):
                scatter(slot, r, n).start()

    def home(slot):
        return send(
            red.at[slot], out.at[mine], t_send.at[slot], t_recv.at[head],
            (lax.rem(z + slot, NZ) * NQ + q, z),
        )

    def reduce(slot):
        value = pbuf[slot, mine].astype(F32)
        for n in range(NH - 1):
            send(
                red.at[slot], rsbuf.at[slot, n],
                rs_send.at[slot, 0, 0], rs_recv.at[slot, n], to_core,
            ).wait_recv()
            value = value + rsbuf[slot, n].astype(F32)
        red[slot] = value.astype(BF16)

    keep = pltpu.make_async_copy(red.at[0], out.at[mine], load_sem.at[len(loads)])

    def go_home(slot):
        if slot > 0:
            home(slot).start()
        else:
            pl.when(z != head)(home(0).start)

            pl.when(z == head)(keep.start)

    def sent_early():
        for way in range(2):
            for step in range(1, last + 1):
                kz(way, step).wait_send()
            kn(way).wait_send()
        for slot in range(NZ):
            for n in range(2):
                kc(slot, n).wait_send()
                if n < len(Y_PIECES):
                    ky(slot, n).wait_send()
                kx(2, slot, n).wait_send()
                if slot not in slots_of(0) + slots_of(1):
                    kx(0, slot, n).wait_send()
                kd(slot, n).wait_send()
        w_core.wait_send()
        w_near.wait_send()
        w_diag.wait_send()

    def sent(slots):
        for slot in slots:
            for r in range(2):
                pl.when(my_r != r)(scatter(slot, r, 0).wait_send)
                for n in range(1, NX):
                    scatter(slot, r, n).wait_send()
            if slot > 0:
                home(slot).wait_send()
            else:
                pl.when(z != head)(home(0).wait_send)
                pl.when(z == head)(keep.wait)

    def finish(slots):
        for slot in slots:
            reduce(slot)
            go_home(slot)

    for r in range(2):
        project((0,), r)
    sent_early()
    for step in range(1, last):
        for r in range(2):
            for way in range(2):
                az(way, step - 1, r).wait_recv()
                az(way, step, r).start()
            project(slots_of(step), r)
            if r == 0 and step > 1:
                finish(slots_of(step - 2))
        for way in range(2):
            for r in range(2):
                az(way, step - 1, r).wait_send()
    for r in range(2):
        for way in range(2):
            az(way, last - 1, r).wait_recv()
        project((last,), r)
    finish(slots_of(last - 2) + slots_of(last - 1) + slots_of(last))
    for n in range(NH):
        there = pl.ds((n // NX + n) % 2 * half + n % NX * part, part)
        arrival = send(red.at[0], out.at[there], t_send.at[0], t_recv.at[n], to_core)
        pl.when(jnp.logical_or(z != head, head != n))(arrival.wait_recv)
    for way in range(2):
        for r in range(2):
            az(way, last - 1, r).wait_send()
    for step in range(last + 1):
        sent(slots_of(step))


def per_device(q_nope, q_rope, latent_keys, kv_gain, up_key, up_value, out_proj, block_order):
    rows = q_nope.shape[0]
    heads = up_key.shape[1] // NOPE
    depth, cols = out_proj.shape
    wide = NQ * cols
    part = rows // NH
    dma = pltpu.SemaphoreType.DMA
    hbm = pl.BlockSpec(memory_space=pl.ANY)
    return pl.pallas_call(
        kernel,
        out_shape=jax.ShapeDtypeStruct((rows, wide), BF16),
        in_specs=[hbm] * 8,
        out_specs=hbm,
        scratch_shapes=[
            pltpu.SMEM(block_order.shape, jnp.int32),
            pltpu.VMEM((LATENT // 128, 128), F32),
            pltpu.VMEM(latent_keys.shape[::-1], BF16),
            pltpu.VMEM(q_nope.shape, BF16),
            pltpu.VMEM(q_rope.shape, BF16),
            pltpu.VMEM(up_key.shape, BF16),
            pltpu.VMEM(up_value.shape, BF16),
            pltpu.VMEM((NQ, cols, depth), BF16),
            pltpu.VMEM((NZ, NQ, WIDTH, rows), BF16),
            pltpu.VMEM((heads * rows, WIDTH), BF16),
            pltpu.VMEM((heads * rows, LATENT), F32),
            pltpu.VMEM((heads * rows, 128), F32),
            pltpu.VMEM((heads * rows, 128), F32),
            pltpu.VMEM((2, rows // 2, rows), F32),
            pltpu.VMEM((NZ, 2, rows // 2, heads * VDIM), BF16),
            pltpu.VMEM((NZ, rows, wide), BF16),
            pltpu.VMEM((NZ, NH - 1, part, wide), BF16),
            pltpu.VMEM((NZ, part, wide), BF16),
            dma((9,)),
            dma((2, NZ // 2)), dma((2, NZ // 2)),
            dma((2,)), dma((2,)),
            dma((2, NZ)), dma((2, NZ)),
            dma((2, NZ)), dma((2, NZ)),
            dma((2, 2, NZ)), dma((2, 2, NZ)),
            dma((2, NZ)), dma((2, NZ)),
            dma((3,)), dma((3,)),
            dma((2, NZ // 2, 2)), dma((2, NZ // 2, 2)),
            dma((NZ, 2, NX)), dma((NZ, NH - 1)),
            dma((NZ,)), dma((NH,)),
            pltpu.SemaphoreType.REGULAR((5,)),
        ],
        compiler_params=pltpu.CompilerParams(
            collective_id=0, has_side_effects=True, vmem_limit_bytes=56 * 1024 * 1024
        ),
    )(
        block_order, kv_gain.reshape(LATENT // 128, 128), latent_keys.T,
        q_nope, q_rope, up_key, up_value, out_proj.T,
    )


def solution(mesh):
    return jax.shard_map(
        per_device,
        mesh=mesh,
        in_specs=(
            P("ctx", "head"),
            P("ctx", "head"),
            P("ctx", None),
            P(),
            P(None, "head"),
            P(None, "head"),
            P("head", "ctx"),
            P(),
        ),
        out_specs=P("ctx", "head"),
        check_vma=False,
    )
```

```python
import math

import jax
import jax.numpy as jnp
from jax import lax
from jax.experimental import pallas as pl
from jax.experimental.pallas import tpu as pltpu
from jax.sharding import PartitionSpec as P

NOPE = 128
ROPE = 64
VDIM = 128
LATENT = 512
CARRIED = LATENT + ROPE
BLOCKS = 64
WIDTH = CARRIED + BLOCKS
NZ = 8
NQ = 4
NX = 4
NH = 8
HIDDEN = -1e30
SCALE = math.log2(math.e) / (NOPE + ROPE) ** 0.5
MESH = pl.DeviceIdType.MESH
F32 = jnp.float32
BF16 = jnp.bfloat16

HALF_WIDTH = CARRIED // 2
Y_PIECES = ((0, 288),)
X_PIECES = ((0, 144), (144, 144))
UNITS = (
    ((0, 0), (0, 2)),
    ((2, 0), (6, 0)),
    ((1, 0), (7, 0)),
    ((3, 0), (5, 0)),
    ((2, 2), (6, 2)),
    ((1, 2), (7, 2)),
    ((3, 2), (5, 2)),
    ((4, 0), (4, 2)),
)


def dot(a, b, dims=((1,), (0,))):
    return lax.dot_general(a, b, (dims, ((), ())), preferred_element_type=F32)


def slots_of(step):
    if step == 0:
        return (0,)
    if step == NZ // 2:
        return (step,)
    return (step, NZ - step)


def pick(table, i):
    value = jnp.int32(table[0])
    for n in range(1, len(table)):
        value = jnp.where(i == n, table[n], value)
    return value


def kernel(
    order_hbm, gain_hbm, latent_hbm, qn_hbm, qr_hbm, upk_hbm, upv_hbm, w_hbm, out,
    order, gain, latent, qn, qr, upk, upv, wbuf, kbuf, qbuf, acc, top, total, tri, abuf, pbuf, rsbuf, red,
    load_sem, kz_send, kz_recv, kn_send, kn_recv, kc_send, kc_recv, ky_send, ky_recv, kx_send, kx_recv,
    kd_send, kd_recv, w_send, w_recv, az_send, az_recv, rs_send, rs_recv, t_send, t_recv, heard,
):
    rows = latent.shape[1]
    half = rows // 2
    heads = upk.shape[1] // NOPE
    cols, depth = w_hbm.shape
    part = rows // NH
    last = NZ // 2
    ctx = lax.axis_index("ctx")
    head = lax.axis_index("head")
    z, q = lax.div(ctx, NQ), lax.rem(ctx, NQ)
    y_lo, core = lax.div(q, 2), lax.rem(q, 2)
    y_hi, x = lax.div(head, NX), lax.rem(head, NX)
    x_odd = lax.rem(x, 2)
    q_core = q + 1 - 2 * core
    q_y = lax.rem(q + 2, NQ)
    q_diag = q_y + 1 - 2 * core
    quads = (q, q_core, q_y, q_diag)

    def along_z(step):
        return lax.rem(z + step + NZ, NZ) * NQ + q, head

    def along_x(step):
        return ctx, y_hi * NX + lax.rem(x + step + NX, NX)

    to_core = (z * NQ + q_core, head)
    to_near = (z * NQ + q_y, head)
    to_far = (z * NQ + q_y, lax.rem(y_hi + 1, 2) * NX + x)

    def send(src, dst, send_sem, recv_sem, device):
        return pltpu.make_async_remote_copy(
            src_ref=src, dst_ref=dst, send_sem=send_sem, recv_sem=recv_sem,
            device_id=device, device_id_type=MESH,
        )

    loads = [
        pltpu.make_async_copy(src, dst, load_sem.at[n])
        for n, (src, dst) in enumerate(
            (
                (latent_hbm, latent), (gain_hbm, gain), (order_hbm, order), (qn_hbm, qn),
                (upk_hbm, upk), (qr_hbm, qr), (upv_hbm, upv), (w_hbm, wbuf.at[q]),
            )
        )
    ]
    loads[0].start()
    loads[1].start()

    nearest = [along_z(1), along_z(-1), along_z(2), along_z(-2), to_core, to_near, to_far]
    nearest += [along_x(1), along_x(-1)]
    barrier = pltpu.get_barrier_semaphore()
    for device in nearest:
        pl.semaphore_signal(barrier, inc=1, device_id=device, device_id_type=MESH)
    rounds = ((to_near, to_far), nearest[7:], nearest[7:], nearest[:4], nearest[2:4])

    def tell(n):
        for device in rounds[n]:
            pl.semaphore_signal(heard.at[n], inc=1, device_id=device, device_id_type=MESH)

    def hear(n):
        pl.semaphore_wait(heard.at[n], len(rounds[n]))
        if n + 1 < len(rounds):
            tell(n + 1)

    for load in loads[2:]:
        load.start()
    loads[0].wait()
    loads[1].wait()
    plain = latent[:LATENT].astype(F32)
    inverse = lax.rsqrt(jnp.mean(plain * plain, axis=0, keepdims=True) + 1e-06)
    for n in range(LATENT // 128):
        span = slice(n * 128, (n + 1) * 128)
        column = jnp.broadcast_to(gain[n : n + 1], (128, 128)).T
        kbuf[0, 0, span] = (plain[span] * inverse * column).astype(BF16)
    kbuf[0, 0, LATENT:CARRIED] = latent[LATENT:]

    def kept(odd, first, size):
        return pl.ds(pl.multiple_of(odd * HALF_WIDTH + first, 16), size)

    def kz(way, step):
        size = HALF_WIDTH if step < last else HALF_WIDTH // 2
        span = kept(x_odd, way * size if step == last else 0, size)
        hops, gone = (step, 0) if step < 3 else (step - 2, 2)
        source = (NZ - gone) % NZ if way == 0 else gone
        target = NZ - step if way == 0 else step
        return send(
            kbuf.at[source, 0, span], kbuf.at[target, 0, span],
            kz_send.at[way, step - 1], kz_recv.at[way, step - 1], along_z(hops * (1 - 2 * way)),
        )

    def kn(way):
        span = kept(1 - x_odd, 0, HALF_WIDTH)
        target = NZ - 1 if way == 0 else 1
        return send(
            kbuf.at[0, 0, span], kbuf.at[target, 0, span],
            kn_send.at[way], kn_recv.at[way], along_z(1 - 2 * way),
        )

    def kc(slot, n):
        span = kept(x_odd if n == 0 else 1 - x_odd, 0, HALF_WIDTH)
        return send(
            kbuf.at[slot, 0, span], kbuf.at[slot, 1, span],
            kc_send.at[n, slot], kc_recv.at[n, slot], to_core,
        )

    def ky(slot, n):
        span = kept(x_odd, *Y_PIECES[n])
        return send(
            kbuf.at[slot, 0, span], kbuf.at[slot, 2, span],
            ky_send.at[n, slot], ky_recv.at[n, slot], (to_far, to_near)[n],
        )

    def kx(quad, slot, n, coming=False):
        span = kept(1 - x_odd if coming else x_odd, *X_PIECES[n])
        return send(
            kbuf.at[slot, quad, span], kbuf.at[slot, quad, span],
            kx_send.at[quad // 2, n, slot], kx_recv.at[quad // 2, n, slot], along_x(1 - 2 * n),
        )

    def kd(slot, n):
        span = kept(x_odd if n == 0 else 1 - x_odd, 0, HALF_WIDTH)
        return send(
            kbuf.at[slot, 2, span], kbuf.at[slot, 3, span],
            kd_send.at[n, slot], kd_recv.at[n, slot], to_core,
        )

    w_core = send(w_hbm, wbuf.at[q], w_send.at[0], w_recv.at[0], to_core)
    w_near = send(w_hbm, wbuf.at[q], w_send.at[1], w_recv.at[1], to_near)
    w_diag = send(wbuf.at[q_y], wbuf.at[q_y], w_send.at[2], w_recv.at[2], to_core)

    def share(step):
        for slot in slots_of(step):
            for n in range(2):
                if step > 1:
                    kx(0, slot, n).start()
                if n < len(Y_PIECES):
                    ky(slot, n).start()
            kc(slot, 0).start()
            if step == 0:
                kc(slot, 1).start()

    def from_z(step):
        for way in range(2):
            kz(way, step).wait_recv()
            if step == 2:
                kz(way, 3).start()
                kz(way, 4).start()
        if step == 2:
            for way in range(2):
                kn(way).start()
        share(step)

    def from_own_x(step):
        for slot in slots_of(step):
            if step == 1:
                kn(0 if slot > 1 else 1).wait_recv()
            else:
                for n in range(2):
                    kx(0, slot, n, True).wait_recv()
            kc(slot, 1).start()

    def from_y(step):
        for slot in slots_of(step):
            for n in range(len(Y_PIECES)):
                ky(slot, n).wait_recv()
            for n in range(2):
                kx(2, slot, n).start()
            kd(slot, 0).start()

    def from_x(step):
        for slot in slots_of(step):
            for n in range(2):
                kx(2, slot, n, True).wait_recv()
            kd(slot, 1).start()

    def near_core(step):
        for slot in slots_of(step):
            kc(slot, 0).wait_recv()
            kc(slot, 1).wait_recv()

    def far_core(step):
        for slot in slots_of(step):
            kd(slot, 0).wait_recv()
            kd(slot, 1).wait_recv()

    pl.semaphore_wait(barrier, len(nearest))
    for step in (2, 1):
        for way in range(2):
            kz(way, step).start()
    share(0)
    w_near.start()
    tell(0)

    loads[2].wait()

    which = lax.broadcasted_iota(jnp.int32, (BLOCKS, rows), 0)
    first_half = lax.broadcasted_iota(jnp.int32, (BLOCKS, rows), 1) < half

    def mark(slot, carry):
        from_z = lax.rem(z + slot, NZ) * NQ
        for n, quad in enumerate(quads):
            there = 2 * (from_z + quad)
            owner = jnp.where(first_half, order[there], order[there + 1])
            kbuf[slot, n, CARRIED:] = jnp.where(which == owner, 1.0, 0.0).astype(BF16)
        return carry

    lax.fori_loop(0, NZ, mark, 0)
    lane = lax.broadcasted_iota(jnp.int32, (half, BLOCKS), 1)
    for r in range(2):
        row = lax.broadcasted_iota(jnp.int32, (half, rows), 0)
        key = lax.broadcasted_iota(jnp.int32, (half, rows), 1) - r * half
        tri[r] = jnp.where(jnp.logical_and(key > row, key < half), HIDDEN, 0.0)
    acc[...] = jnp.zeros_like(acc)
    total[...] = jnp.zeros_like(total)
    top[...] = jnp.full_like(top, HIDDEN)

    loads[3].wait()
    loads[4].wait()
    loads[5].wait()
    for n in range(heads):
        own = slice(n * NOPE, (n + 1) * NOPE)
        turned = dot(qn[:, own], upk[:, own], ((1,), (1,))).astype(BF16)
        rope = qr[:, n * ROPE : (n + 1) * ROPE]
        for r in range(2):
            span = slice((r * heads + n) * half, (r * heads + n + 1) * half)
            mine = slice(r * half, (r + 1) * half)
            later = jnp.where(lane > order[2 * ctx + r], HIDDEN, 0.0).astype(BF16)
            qbuf[span, :LATENT] = turned[mine]
            qbuf[span, LATENT:] = jnp.concatenate([rope[mine], later], axis=1)

    from_y(0)
    from_z(2)
    from_x(0)
    from_z(1)
    hear(0)

    def before_0():
        near_core(0)
        far_core(0)

    def before_1():
        from_own_x(2)
        from_z(3)
        from_y(2)
        near_core(2)
        w_core.start()
        hear(1)

    def before_2():
        from_z(4)
        from_own_x(1)
        from_y(1)
        from_own_x(3)
        near_core(1)
        hear(2)

    def before_3():
        from_y(3)
        from_x(2)
        from_y(4)
        near_core(3)
        hear(3)

    def before_4():
        w_near.wait_recv()
        w_diag.start()
        from_own_x(4)
        from_x(1)
        far_core(2)

    def before_5():
        from_x(3)
        from_x(4)
        far_core(1)
        hear(4)

    befores = (before_0, before_1, before_2, before_3, before_4)
    chunk = heads * half

    def soft(span, score, block):
        keys = score.shape[1]
        before = top[span]
        peak = jnp.maximum(before, jnp.max(score, axis=1, keepdims=True))
        fade = jnp.exp2((before - peak) * SCALE)
        expo = jnp.exp2((score - jnp.concatenate([peak] * (keys // 128), axis=1)) * SCALE)
        added = expo[:, :128]
        for n in range(1, keys // 128):
            added = added + expo[:, n * 128 : (n + 1) * 128]
        total[span] = total[span] * fade + added
        top[span] = peak
        faded = acc[span] * jnp.concatenate([fade] * (LATENT // 128), axis=1)
        acc[span] = faded + dot(expo.astype(BF16), block[:LATENT], ((1,), (1,)))

    def attend(i, carry):
        for n, before in enumerate(befores):
            pl.when(i == n)(before)
        pairs = [[pick([u[m][n] for u in UNITS], i) for n in range(2)] for m in range(2)]
        block = jnp.concatenate([kbuf[s, quad + n] for s, quad in pairs for n in range(2)], axis=1)
        spans = [slice(r * chunk, (r + 1) * chunk) for r in range(2)]
        scores = [dot(qbuf[span], block) for span in spans]
        for r in range(2):
            score = scores[r]
            own = (score[:, :rows].reshape(heads, half, rows) + tri[r][None]).reshape(chunk, rows)
            soft(spans[r], jnp.concatenate([own, score[:, rows:]], axis=1), block)

        @pl.when(i == 0)
        def _():
            tri[...] = jnp.zeros_like(tri)

        return carry

    lax.fori_loop(0, len(befores), attend, 0)
    before_5()
    loads[6].wait()
    loads[7].wait()

    def blocks(units):
        return jnp.concatenate(
            [kbuf[s, quad + n] for u in units for s, quad in u for n in range(2)], axis=1
        )

    ahead = len(befores)
    block = blocks(UNITS[ahead : ahead + 1])
    soft(slice(0, chunk), dot(qbuf[:chunk], block), block)
    near_core(4)
    far_core(3)
    far_core(4)

    def az(way, step, r):
        source = (NZ - step) % NZ if way == 0 else step
        target = (NZ - step - 1) % NZ if way == 0 else step + 1
        src, dst = abuf.at[source, r], abuf.at[target, r]
        if step == last - 1:
            span = pl.ds(way * (half // 2), half // 2)
            src, dst = src.at[span], dst.at[span]
        return send(
            src, dst, az_send.at[way, step, r], az_recv.at[way, step, r], along_z(1 - 2 * way),
        )

    for r in range(2):
        span = slice(r * chunk, (r + 1) * chunk)
        block = blocks(UNITS[ahead + 1 - r :])
        soft(span, dot(qbuf[span], block), block)
        for n in range(heads):
            mine = slice((r * heads + n) * half, (r * heads + n + 1) * half)
            own = slice(n * VDIM, (n + 1) * VDIM)
            wide = acc[mine]
            high = wide.astype(BF16)
            low = (wide - high.astype(F32)).astype(BF16)
            summed = dot(high, upv[:, own]) + dot(low, upv[:, own])
            weight = jnp.sum(total[mine], axis=1, keepdims=True)
            abuf[0, r, :, own] = (summed / weight).astype(BF16)
        az(0, 0, r).start()
        az(1, 0, r).start()

    w_core.wait_recv()
    w_diag.wait_recv()

    my_r = lax.rem(y_hi + x, 2)
    mine = pl.ds(pl.multiple_of(my_r * half + x * part, part), part)

    def scatter(slot, r, n):
        k = lax.rem(x + n, NX)
        owner_y = lax.rem(k + r, 2)
        other = lax.rem(owner_y + y_hi, 2)
        there = pl.ds(pl.multiple_of(r * half + k * part, part), part)
        place = n - 1 + NX * other if n > 0 else NX - 1
        return send(
            pbuf.at[slot, there], rsbuf.at[slot, place],
            rs_send.at[slot, r, n], rs_recv.at[slot, place], (ctx, owner_y * NX + k),
        )

    def project(slots, r):
        made = jnp.concatenate([abuf[slot, r] for slot in slots], axis=0)
        made = dot(made, wbuf[...].reshape(NQ * cols, depth), ((1,), (1,))).astype(BF16)
        for n, slot in enumerate(slots):
            pbuf[slot, r * half : (r + 1) * half] = made[n * half : (n + 1) * half]
        for slot in slots:
            pl.when(my_r != r)(scatter(slot, r, 0).start)
            for n in range(1, NX):
                scatter(slot, r, n).start()

    def home(slot):
        return send(
            red.at[slot], out.at[mine], t_send.at[slot], t_recv.at[head],
            (lax.rem(z + slot, NZ) * NQ + q, z),
        )

    def reduce(slot):
        value = pbuf[slot, mine].astype(F32)
        for n in range(NH - 1):
            send(
                red.at[slot], rsbuf.at[slot, n],
                rs_send.at[slot, 0, 0], rs_recv.at[slot, n], to_core,
            ).wait_recv()
            value = value + rsbuf[slot, n].astype(F32)
        red[slot] = value.astype(BF16)

    keep = pltpu.make_async_copy(red.at[0], out.at[mine], load_sem.at[len(loads)])

    def go_home(slot):
        if slot > 0:
            home(slot).start()
        else:
            pl.when(z != head)(home(0).start)

            pl.when(z == head)(keep.start)

    def sent_early():
        for way in range(2):
            for step in range(1, last + 1):
                kz(way, step).wait_send()
            kn(way).wait_send()
        for slot in range(NZ):
            for n in range(2):
                kc(slot, n).wait_send()
                if n < len(Y_PIECES):
                    ky(slot, n).wait_send()
                kx(2, slot, n).wait_send()
                if slot not in slots_of(0) + slots_of(1):
                    kx(0, slot, n).wait_send()
                kd(slot, n).wait_send()
        w_core.wait_send()
        w_near.wait_send()
        w_diag.wait_send()

    def sent(slots):
        for slot in slots:
            for r in range(2):
                pl.when(my_r != r)(scatter(slot, r, 0).wait_send)
                for n in range(1, NX):
                    scatter(slot, r, n).wait_send()
            if slot > 0:
                home(slot).wait_send()
            else:
                pl.when(z != head)(home(0).wait_send)
                pl.when(z == head)(keep.wait)

    def finish(slots):
        for slot in slots:
            reduce(slot)
            go_home(slot)

    for r in range(2):
        project((0,), r)
    sent_early()
    for step in range(1, last):
        for r in range(2):
            for way in range(2):
                az(way, step - 1, r).wait_recv()
                az(way, step, r).start()
            project(slots_of(step), r)
            if r == 0 and step > 1:
                finish(slots_of(step - 2))
        for way in range(2):
            for r in range(2):
                az(way, step - 1, r).wait_send()
    for r in range(2):
        for way in range(2):
            az(way, last - 1, r).wait_recv()
        project((last,), r)
    finish(slots_of(last - 2) + slots_of(last - 1) + slots_of(last))
    for n in range(NH):
        there = pl.ds((n // NX + n) % 2 * half + n % NX * part, part)
        arrival = send(red.at[0], out.at[there], t_send.at[0], t_recv.at[n], to_core)
        pl.when(jnp.logical_or(z != head, head != n))(arrival.wait_recv)
    for way in range(2):
        for r in range(2):
            az(way, last - 1, r).wait_send()
    for step in range(last + 1):
        sent(slots_of(step))


def per_device(q_nope, q_rope, latent_keys, kv_gain, up_key, up_value, out_proj, block_order):
    rows = q_nope.shape[0]
    heads = up_key.shape[1] // NOPE
    depth, cols = out_proj.shape
    wide = NQ * cols
    part = rows // NH
    dma = pltpu.SemaphoreType.DMA
    hbm = pl.BlockSpec(memory_space=pl.ANY)
    return pl.pallas_call(
        kernel,
        out_shape=jax.ShapeDtypeStruct((rows, wide), BF16),
        in_specs=[hbm] * 8,
        out_specs=hbm,
        scratch_shapes=[
            pltpu.SMEM(block_order.shape, jnp.int32),
            pltpu.VMEM((LATENT // 128, 128), F32),
            pltpu.VMEM(latent_keys.shape[::-1], BF16),
            pltpu.VMEM(q_nope.shape, BF16),
            pltpu.VMEM(q_rope.shape, BF16),
            pltpu.VMEM(up_key.shape, BF16),
            pltpu.VMEM(up_value.shape, BF16),
            pltpu.VMEM((NQ, cols, depth), BF16),
            pltpu.VMEM((NZ, NQ, WIDTH, rows), BF16),
            pltpu.VMEM((heads * rows, WIDTH), BF16),
            pltpu.VMEM((heads * rows, LATENT), F32),
            pltpu.VMEM((heads * rows, 128), F32),
            pltpu.VMEM((heads * rows, 128), F32),
            pltpu.VMEM((2, rows // 2, rows), F32),
            pltpu.VMEM((NZ, 2, rows // 2, heads * VDIM), BF16),
            pltpu.VMEM((NZ, rows, wide), BF16),
            pltpu.VMEM((NZ, NH - 1, part, wide), BF16),
            pltpu.VMEM((NZ, part, wide), BF16),
            dma((9,)),
            dma((2, NZ // 2)), dma((2, NZ // 2)),
            dma((2,)), dma((2,)),
            dma((2, NZ)), dma((2, NZ)),
            dma((2, NZ)), dma((2, NZ)),
            dma((2, 2, NZ)), dma((2, 2, NZ)),
            dma((2, NZ)), dma((2, NZ)),
            dma((3,)), dma((3,)),
            dma((2, NZ // 2, 2)), dma((2, NZ // 2, 2)),
            dma((NZ, 2, NX)), dma((NZ, NH - 1)),
            dma((NZ,)), dma((NH,)),
            pltpu.SemaphoreType.REGULAR((5,)),
        ],
        compiler_params=pltpu.CompilerParams(
            collective_id=0, has_side_effects=True, vmem_limit_bytes=56 * 1024 * 1024
        ),
    )(
        block_order, kv_gain.reshape(LATENT // 128, 128), latent_keys.T,
        q_nope, q_rope, up_key, up_value, out_proj.T,
    )


def solution(mesh):
    return jax.shard_map(
        per_device,
        mesh=mesh,
        in_specs=(
            P("ctx", "head"),
            P("ctx", "head"),
            P("ctx", None),
            P(),
            P(None, "head"),
            P(None, "head"),
            P("head", "ctx"),
            P(),
        ),
        out_specs=P("ctx", "head"),
        check_vma=False,
    )
```
